128 devices in a mesh: ctx: 32 (over x, z, y_hi), tp: 4 (over y_lo, core).
Axes of the slice: x: 4, y: 4 (y_hi: 2, y_lo: 2; y = y_hi * 2 + y_lo), z: 4, core: 2. Of those that a mesh axis runs over, the one named last changes fastest.
Arguments:
- queries: bfloat16 [4, 4096, 4096], P('tp', 'ctx')
- attn_keys: bfloat16 [4, 4096, 512], P('tp', 'ctx')
- hidden: bfloat16 [4, 4096, 5120], P('tp', 'ctx'), may hold values from -6 to 6
- out_grad: bfloat16 [4, 4096, 4096], P('tp', 'ctx'), may hold values from -6 to 6
- logp_new: float32 [4, 4096], P('tp', 'ctx'), may hold values from -1.2 to -0.2
- logp_old: float32 [4, 4096], P('tp', 'ctx'), may hold values from -1.2 to -0.2
- logp_ref: float32 [4, 4096], P('tp', 'ctx'), may hold values from -3 to -0.05
- lengths: int32 [4, 2], P('tp'), may hold values from 1 to 3584, 4096 in all within a row
- rewards: float32 [4, 2], replicated, may hold values from -4 to 4
- groups: int32 [4, 2], replicated, may hold values from 0 to 1, as said below
- master: float32 [5120, 512], P(('ctx', 'tp')), may hold values from -0.078125 to 0.078125
- first_moment: float32 [5120, 512], P(('ctx', 'tp')), may hold values from -3 to 3
- second_moment: float32 [5120, 512], P(('ctx', 'tp')), may hold values from 0.1 to 1
- dec_hidden: bfloat16 [4, 1024, 5120], P(None, 'ctx'), may hold values from -6 to 6
- dec_query: bfloat16 [4, 1024, 4096], P(None, 'ctx', 'tp')
- dec_key: bfloat16 [4, 1024, 512], P(None, 'ctx', 'tp'), may hold values from -16 to 16
- cache_keys: bfloat16 [1024, 512, 512], P('ctx', None, 'tp')
- cache_values: bfloat16 [1024, 512, 512], P('ctx', None, 'tp'), may hold values from -6 to 6
- cache_len: int32 [1024], P('ctx'), may hold values from 1 to 508, as said below
- out_weight: bfloat16 [4096, 5120], P('tp'), may hold values from -0.5 to 0.5
Outputs:
- new_master: float32 [5120, 512], P(('ctx', 'tp'))
- new_first: float32 [5120, 512], P(('ctx', 'tp'))
- new_second: float32 [5120, 512], P(('ctx', 'tp'))
- rollout_weights: bfloat16 [5120, 512], P(None, 'tp')
- dec_out: bfloat16 [4, 1024, 5120], P(None, 'ctx')
The draws below stay inside these ranges and needn't reach their ends.
Inputs may be any that keep to these rules, and one draw needn't show every extreme that they name: `groups`: each of the 2 prompts is named by exactly 4 rollouts. `cache_len`: in the 32 rows of each device group one row has 508 filled positions.
All inputs are finite; a program needn't handle non-finite values.
Results may differ from the reference program's by a relative error of at most 0.0067.
Values may be sent and summed in bfloat16 or wider, within the bound.
No kernel may reach another device: no remote copies, remote signals or barrier semaphores. Data moves between devices by JAX's collectives and lax.ppermute only.
A program may use at most 128 MiB of HBM per device.

```python
import math
import jax
import jax.numpy as jnp
import numpy as np
from jax import lax

D = 5120
HD = 128
HEADS = 32
KV = 4
SLAB = 4096
SEQS = 4
ROLL = 2
PROMPTS = 2
ROWS_DEV = 32
ROWS = 1024
CACHE = 512
STEPS = 4


def slab_key_base(key):
    return jax.random.truncated_normal(key, -6.0, 6.0, (SEQS, SLAB, KV * HD), jnp.float32)


def cache_key_base(key):
    return jax.random.truncated_normal(key, -6.0, 6.0, (ROWS, CACHE, KV * HD), jnp.float32)


def draw_attn_keys(key, part):
    return slab_key_base(key).astype(jnp.bfloat16)


def draw_queries(key, part):
    key = jax.random.fold_in(key, 7)
    key_noise = jax.random.fold_in(key, 0)
    values = jax.random.truncated_normal(key_noise, -6.0, 6.0, (SEQS, SLAB, HEADS * HD), jnp.float32)
    return values.astype(jnp.bfloat16)


def draw_cache_keys(key, part):
    return cache_key_base(key).astype(jnp.bfloat16)


def draw_dec_query(key, part):
    key = jax.random.fold_in(key, 13)
    key_noise = jax.random.fold_in(key, 0)
    values = jax.random.truncated_normal(key_noise, -6.0, 6.0, (STEPS, ROWS, HEADS * HD), jnp.float32)
    return values.astype(jnp.bfloat16)


def draw_groups(key, part):
    key = jax.random.fold_in(key, 29)
    order = jax.random.permutation(key, SEQS * ROLL)
    return (order % PROMPTS).reshape(SEQS, ROLL).astype(jnp.int32)


def draw_cache_len(key, part):
    key = jax.random.fold_in(key, 19)
    key_len, key_slot = jax.random.split(key)
    most_len = CACHE - STEPS
    base_len = jax.random.randint(key_len, (ROWS,), 1, most_len + 1)
    slot = jax.random.randint(key_slot, (ROWS // ROWS_DEV, 1), 0, ROWS_DEV)
    filled = (jnp.arange(ROWS_DEV)[None, :] == slot).reshape(ROWS)
    return jnp.where(filled, most_len, base_len).astype(jnp.int32)


def level_of(own_key, extent, cuts, low, top_value):
    loudness = 1.0
    for axis_at, shards_of in cuts:
        draws = jax.random.uniform(jax.random.fold_in(jax.random.fold_in(own_key, 6), axis_at), (shards_of,), jnp.float32, low / len(cuts), top_value / len(cuts))
        loudness = loudness * jnp.repeat(jnp.exp(draws), extent[axis_at] // shards_of).reshape((-1,) + (1,) * (len(extent) - 1 - axis_at))
    return loudness


def profile(amount, total, most, skew):
    weights = [(1 << 20) // math.isqrt(standing ** skew) + 1 for standing in range(2, amount + 1)]
    rest, counts = total - most - (amount - 1), [1] * (amount - 1)
    while rest > 0:
        candidates = [i for i in range(amount - 1) if counts[i] < most]
        pool, remaining = sum([weights[i] for i in candidates]), rest
        for i in candidates:
            addition = min(most - counts[i], max(1, remaining * weights[i] // pool), rest)
            counts[i] = counts[i] + addition
            rest = rest - addition
    return np.array([most] + counts)


def ragged_sizes(rng, amount, total, limit, slope):
    if amount == 2:
        one = jax.random.randint(rng, (), max(1, total - limit), min(limit, total - 1) + 1)
        return jnp.stack([one, total - one])
    tallies = jnp.asarray(profile(amount, total, limit, slope), jnp.int32)
    pairs = (amount - 1) // 2
    giver, sink = tallies[1:1 + 2 * pairs:2], tallies[2:2 + 2 * pairs:2]
    slack = jnp.minimum(giver - 1, limit - sink)
    shifted = jax.random.randint(jax.random.fold_in(rng, 1), (pairs,), 0, 1 << 20) % (slack + 1)
    tallies = tallies.at[1:1 + 2 * pairs:2].set(giver - shifted).at[2:2 + 2 * pairs:2].set(sink + shifted)
    return tallies[jax.random.permutation(jax.random.fold_in(rng, 2), amount)]


def bell_draw(key, extent, deviation, most, cuts=(), kind=jnp.bfloat16):
    entries = jax.random.normal(key, extent, jnp.float32) * deviation
    if len(cuts) > 0:
        entries = level_of(key, extent, cuts, -0.22, 0.18) * entries
    return jnp.clip(entries, min=-most, max=most).astype(kind)


def setup_inputs(seed: int = 0) -> dict:
    splits = jax.random.split(jax.random.key(seed), 21)
    queries = draw_queries(jax.random.fold_in(splits[20], 71), 0)
    attn_keys = draw_attn_keys(jax.random.fold_in(splits[20], 71), 0)
    hidden = bell_draw(splits[2], (SEQS, SLAB, D), 1.0, 6.0, ((0, 4), (1, 32)))
    out_grad = bell_draw(splits[3], (SEQS, SLAB, HEADS * HD), 1.0, 6.0, ((0, 4), (1, 32)))
    logp_new = jnp.clip(-1.2 + 1 * jax.random.uniform(splits[4], (SEQS, SLAB), jnp.float32) ** level_of(splits[4], (SEQS, SLAB), ((0, 4), (1, 32)), -0.2, 0.2), -1.2, -0.2)
    logp_old = jnp.clip(-1.2 + 1 * jax.random.uniform(splits[5], (SEQS, SLAB), jnp.float32) ** level_of(splits[5], (SEQS, SLAB), ((0, 4), (1, 32)), -0.2, 0.2), -1.2, -0.2)
    logp_ref = jnp.clip(-3.0 + 2.95 * jax.random.uniform(splits[6], (SEQS, SLAB), jnp.float32) ** level_of(splits[6], (SEQS, SLAB), ((0, 4), (1, 32)), -0.2, 0.2), -3.0, -0.05)
    lengths = jax.vmap(lambda own: ragged_sizes(own, ROLL, SLAB, SLAB - SLAB // 8, 1))(jax.random.split(splits[7], SEQS)).reshape((SEQS, ROLL)).astype(jnp.int32)
    rewards = bell_draw(splits[8], (SEQS, ROLL), 1.0, 4.0, (), jnp.float32)
    groups = draw_groups(jax.random.fold_in(splits[20], 71), 0)
    master = bell_draw(splits[10], (D, KV * HD), D ** -0.5, 0.078125, ((0, 128),), jnp.float32)
    first_moment = bell_draw(splits[11], (D, KV * HD), 0.5, 3.0, ((0, 128),), jnp.float32)
    second_moment = jnp.clip(jnp.exp(math.log(1.0) - 2.3025851 * jax.random.uniform(splits[12], (D, KV * HD), jnp.float32) ** level_of(splits[12], (D, KV * HD), ((0, 128),), -0.2, 0.2)), 0.1, 1.0)
    dec_hidden = bell_draw(splits[13], (STEPS, ROWS, D), 1.0, 6.0, ((1, 32),))
    dec_query = draw_dec_query(jax.random.fold_in(splits[20], 71), 0)
    dec_key = bell_draw(splits[15], (STEPS, ROWS, KV * HD), 3.0, 16.0, ((1, 32), (2, 4)))
    cache_keys = draw_cache_keys(jax.random.fold_in(splits[20], 71), 0)
    cache_values = bell_draw(splits[17], (ROWS, CACHE, KV * HD), 1.0, 6.0, ((0, 32), (2, 4)))
    cache_len = draw_cache_len(jax.random.fold_in(splits[20], 71), 0)
    out_weight = bell_draw(splits[19], (HEADS * HD, D), HD ** -0.5, 0.5, ((0, 4),))
    return dict(queries=queries, attn_keys=attn_keys, hidden=hidden, out_grad=out_grad, logp_new=logp_new, logp_old=logp_old, logp_ref=logp_ref, lengths=lengths, rewards=rewards, groups=groups, master=master, first_moment=first_moment, second_moment=second_moment, dec_hidden=dec_hidden, dec_query=dec_query, dec_key=dec_key, cache_keys=cache_keys, cache_values=cache_values, cache_len=cache_len, out_weight=out_weight)


first_decay = 0.9
second_decay = 0.95
adam_eps = 1e-08
learn_rate = 0.001
decay_weight = 0.1
kl_weight = 0.1

def segment_ids(lengths_row, position):
    doc_ends = jnp.cumsum(lengths_row).astype(jnp.int32)
    return lax.optimization_barrier(jnp.sum((position[:, None] >= doc_ends[None, :]).astype(jnp.int32), axis=1))

def group_advantage(rewards, groups):
    flat_reward = rewards.reshape(-1)
    flat_group = groups.reshape(-1)
    same_group = (flat_group[:, None] == flat_group[None, :]).astype(jnp.float32)
    group_mean = lax.optimization_barrier(jnp.sum(same_group * flat_reward[None, :], axis=1)) / lax.optimization_barrier(jnp.sum(same_group, axis=1))
    return (flat_reward - group_mean).reshape(rewards.shape)

def token_coef(own_advantage, segment, policy_logp, sample_logp, frozen_logp, divisor):
    labels = jnp.arange(own_advantage.shape[0], dtype=jnp.int32)
    picked = lax.optimization_barrier(jnp.sum(jnp.where(segment[:, None] == labels[None, :], own_advantage[None, :], 0.0), axis=1))
    return (-jnp.exp(policy_logp - sample_logp) * picked + kl_weight * (1.0 - jnp.exp(frozen_logp - policy_logp))) / divisor

def value_grad(query_slab, key_slab, dout_slab, segment):
    group_size = HEADS // KV
    score_scale = HD ** (-0.5)
    query_heads = query_slab.astype(jnp.float32).reshape(SLAB, KV, group_size, HD)
    key_heads = key_slab.astype(jnp.float32).reshape(SLAB, KV, HD)
    dout_heads = dout_slab.astype(jnp.float32).reshape(SLAB, KV, group_size, HD)
    block_rows = math.gcd(SLAB, 256)
    position = jnp.arange(SLAB, dtype=jnp.int32)

    def one_block(running, block_index):
        first_row = block_index * block_rows
        query_block = lax.dynamic_slice_in_dim(query_heads, first_row, block_rows, 0)
        dout_block = lax.dynamic_slice_in_dim(dout_heads, first_row, block_rows, 0)
        query_position = first_row + jnp.arange(block_rows, dtype=jnp.int32)
        query_segment = lax.dynamic_slice_in_dim(segment, first_row, block_rows, 0)
        visible = (position[None, :] <= query_position[:, None]) & (segment[None, :] == query_segment[:, None])
        visible = visible[:, None, None, :]
        scores = jnp.einsum('tkgd,ckd->tkgc', query_block, key_heads) * score_scale
        row_max = lax.optimization_barrier(jnp.max(jnp.where(visible, scores, -jnp.inf), axis=3, keepdims=True))
        log_total = row_max + jnp.log(lax.optimization_barrier(jnp.sum(jnp.where(visible, jnp.exp(scores - row_max), 0.0), axis=3, keepdims=True)))
        weights = jnp.where(visible, jnp.exp(scores - log_total), 0.0).astype(jnp.bfloat16)
        running = running + jnp.einsum('tkgc,tkgd->ckd', weights.astype(jnp.float32), dout_block)
        return (running, None)
    summed, _ = lax.scan(one_block, jnp.zeros((SLAB, KV, HD), jnp.float32), jnp.arange(SLAB // block_rows, dtype=jnp.int32))
    return summed.reshape(SLAB, KV * HD).astype(jnp.bfloat16)

def decode_step(step_index, dec_query, dec_key, fresh_values, cache_keys, cache_values, cache_len):
    group_size = HEADS // KV
    score_scale = HD ** (-0.5)
    query_now = lax.dynamic_index_in_dim(dec_query, step_index, 0, keepdims=False)
    query_heads = query_now.astype(jnp.float32).reshape(ROWS, KV, group_size, HD)
    old_keys = cache_keys.astype(jnp.float32).reshape(ROWS, CACHE, KV, HD)
    old_values = cache_values.astype(jnp.float32).reshape(ROWS, CACHE, KV, HD)
    fresh_keys = dec_key.astype(jnp.float32).reshape(STEPS, ROWS, KV, HD)
    fresh_vals = fresh_values.astype(jnp.float32).reshape(STEPS, ROWS, KV, HD)
    old_scores = jnp.einsum('rkgd,rckd->rkgc', query_heads, old_keys) * score_scale
    new_scores = jnp.einsum('rkgd,jrkd->rkgj', query_heads, fresh_keys) * score_scale
    old_visible = (jnp.arange(CACHE, dtype=jnp.int32)[None, :] < cache_len[:, None])[:, None, None, :]
    new_visible = (jnp.arange(STEPS, dtype=jnp.int32) <= step_index)[None, None, None, :]
    row_max = jnp.maximum(lax.optimization_barrier(jnp.max(jnp.where(old_visible, old_scores, -jnp.inf), axis=3)), lax.optimization_barrier(jnp.max(jnp.where(new_visible, new_scores, -jnp.inf), axis=3)))[..., None]
    old_exp = jnp.where(old_visible, jnp.exp(old_scores - row_max), 0.0)
    new_exp = jnp.where(new_visible, jnp.exp(new_scores - row_max), 0.0)
    denom = lax.optimization_barrier(jnp.sum(old_exp, axis=3, keepdims=True)) + lax.optimization_barrier(jnp.sum(new_exp, axis=3, keepdims=True))
    old_weights = (old_exp / denom).astype(jnp.bfloat16).astype(jnp.float32)
    new_weights = (new_exp / denom).astype(jnp.bfloat16).astype(jnp.float32)
    attended = jnp.einsum('rkgc,rckd->rkgd', old_weights, old_values) + jnp.einsum('rkgj,jrkd->rkgd', new_weights, fresh_vals)
    return attended.reshape(ROWS, HEADS * HD).astype(jnp.bfloat16)

def reference(queries, attn_keys, hidden, out_grad, logp_new, logp_old, logp_ref, lengths, rewards, groups, master, first_moment, second_moment, dec_hidden, dec_query, dec_key, cache_keys, cache_values, cache_len, out_weight):
    advantage = group_advantage(rewards, groups)
    position = jnp.arange(SLAB, dtype=jnp.int32)
    gradient = jnp.zeros((D, KV * HD), jnp.float32)
    for slab_index in range(SEQS):
        segment = segment_ids(lengths[slab_index], position)
        token_weight = token_coef(advantage[slab_index], segment, logp_new[slab_index], logp_old[slab_index], logp_ref[slab_index], float(SEQS * ROLL))
        dout_rows = (token_weight[:, None] * out_grad[slab_index].astype(jnp.float32)).astype(jnp.bfloat16)
        dvalue = value_grad(queries[slab_index], attn_keys[slab_index], dout_rows, segment)
        gradient = gradient + lax.dot_general(hidden[slab_index], dvalue, (((0,), (0,)), ((), ())), preferred_element_type=jnp.float32)
    new_first = first_decay * first_moment + (1.0 - first_decay) * gradient
    new_second = second_decay * second_moment + (1.0 - second_decay) * gradient * gradient
    new_master = master - learn_rate * (new_first / (jnp.sqrt(new_second) + adam_eps) + decay_weight * master)
    rollout_weights = new_master.astype(jnp.bfloat16)
    fresh_values = jnp.dot(dec_hidden.reshape(STEPS * ROWS, D), rollout_weights, preferred_element_type=jnp.float32)
    fresh_values = fresh_values.reshape(STEPS, ROWS, KV * HD).astype(jnp.bfloat16)

    def one_step(step_index):
        return decode_step(step_index, dec_query, dec_key, fresh_values, cache_keys, cache_values, cache_len)
    attended = lax.map(one_step, jnp.arange(STEPS, dtype=jnp.int32))
    dec_out = jnp.dot(attended.reshape(STEPS * ROWS, HEADS * HD), out_weight, preferred_element_type=jnp.float32)
    dec_out = dec_out.astype(jnp.bfloat16).reshape(STEPS, ROWS, D)
    return (new_master, new_first, new_second, rollout_weights, dec_out)
```

```python
import math

import jax
import jax.numpy as jnp
from jax import lax
from jax.experimental import pallas as pl
from jax.experimental.pallas import tpu as pltpu
from jax.sharding import PartitionSpec as P

HD = 128
HEADS = 32
KV = 4
GROUP = HEADS // KV
BLOCK = 128
NX, NZ, NY, NT = 4, 4, 2, 4
NG = NZ * NY
SLAB = NX * NG * BLOCK
CHUNK = 512
ROWS = GROUP * BLOCK
LOWEST = -1e30

first_decay = 0.9
second_decay = 0.95
adam_eps = 1e-08
learn_rate = 0.001
decay_weight = 0.1
kl_weight = 0.1
exp2_scale = HD ** (-0.5) * math.log2(math.e)


def route(value, target):
    pairs = []
    for source in range(NX * NG * NT):
        ctx, t = divmod(source, NT)
        x, g = divmod(ctx, NG)
        z, y = divmod(g, NY)
        nx, nz, ny, nt = target(x, z, y, t)
        pairs.append((source, (((nx % NX) * NZ + nz % NZ) * NY + ny % NY) * NT + nt % NT))
    return lax.ppermute(value, ("ctx", "tp"), pairs)


def pick(value, index, axis=0):
    return lax.dynamic_index_in_dim(value, index, axis, keepdims=False)


def segment_ids(lengths_row, position):
    doc_ends = jnp.cumsum(lengths_row)
    return jnp.sum((position[:, None] >= doc_ends[None, :]).astype(jnp.int32), axis=1)


def group_advantage(rewards, groups):
    flat_reward = rewards.reshape(-1)
    flat_group = groups.reshape(-1)
    same_group = (flat_group[:, None] == flat_group[None, :]).astype(jnp.float32)
    group_mean = jnp.sum(same_group * flat_reward[None, :], axis=1) / jnp.sum(same_group, axis=1)
    return (flat_reward - group_mean).reshape(rewards.shape)


def token_coef(own_advantage, segment, policy_logp, sample_logp, frozen_logp, divisor):
    labels = jnp.arange(own_advantage.shape[0], dtype=jnp.int32)
    picked = jnp.sum(
        jnp.where(segment[:, None] == labels[None, :], own_advantage[None, :], 0.0), axis=1
    )
    return (
        -jnp.exp(policy_logp - sample_logp) * picked
        + kl_weight * (1.0 - jnp.exp(frozen_logp - policy_logp))
    ) / divisor


def heads_as_rows(block):
    return jnp.concatenate([block[:, h * HD : (h + 1) * HD] for h in range(GROUP)], axis=0)


def chunk_range(block_start, bound):
    seen_from = jnp.where(block_start >= bound, bound, 0)
    first = seen_from // CHUNK
    stop = (block_start + BLOCK - 1) // CHUNK + 1
    return first, stop


def chunk_hidden(chunk_start, block_start, bound):
    key_at = chunk_start + lax.broadcasted_iota(jnp.int32, (CHUNK, ROWS), 0)
    query_at = block_start + (lax.broadcasted_iota(jnp.int32, (1, ROWS), 1) & (BLOCK - 1))
    from_at = jnp.where(query_at >= bound, bound, 0)
    return (key_at <= query_at) & (key_at >= from_at)


def chunk_whole(chunk_start, block_start, bound):
    latest_from = jnp.where(block_start + BLOCK - 1 >= bound, bound, 0)
    return (chunk_start + CHUNK - 1 <= block_start) & (chunk_start >= latest_from)


def fill_keys(where_ref, keys_ref, key_rows):
    head = where_ref[1]
    for x in range(NX):
        slot = lax.rem(head - x + NX, NX)
        for g in range(NG):
            key_rows[pl.ds((x * NG + g) * BLOCK, BLOCK), :] = keys_ref[g, slot]


def totals_kernel(where_ref, queries_ref, keys_ref, total_ref, key_rows, score_ref):
    g, head, bound = where_ref[0], where_ref[1], where_ref[2]
    fill_keys(where_ref, keys_ref, key_rows)

    def one_block(slot, _):
        block_start = (lax.rem(head - slot + NX, NX) * NG + g) * BLOCK
        query_rows = heads_as_rows(queries_ref[slot])
        first, stop = chunk_range(block_start, bound)

        def one_chunk(chunk, state):
            running_max, running_sum = state
            chunk_start = pl.multiple_of(chunk * CHUNK, CHUNK)
            score_ref[...] = lax.dot_general(
                key_rows[pl.ds(chunk_start, CHUNK), :],
                query_rows,
                (((1,), (1,)), ((), ())),
                preferred_element_type=jnp.float32,
            )

            @pl.when(jnp.logical_not(chunk_whole(chunk_start, block_start, bound)))
            def _():
                visible = chunk_hidden(chunk_start, block_start, bound)
                score_ref[...] = jnp.where(visible, score_ref[...], LOWEST)

            scores = score_ref[...]
            new_max = jnp.maximum(
                running_max, jnp.max(scores, axis=0, keepdims=True) * exp2_scale
            )
            running_sum = running_sum * jnp.exp2(running_max - new_max) + jnp.sum(
                jnp.exp2(scores * exp2_scale - new_max), axis=0, keepdims=True
            )
            return new_max, running_sum

        row_max, row_sum = lax.fori_loop(
            first,
            stop,
            one_chunk,
            (jnp.full((1, ROWS), LOWEST, jnp.float32), jnp.zeros((1, ROWS), jnp.float32)),
        )
        total_ref[slot] = row_max + jnp.log2(row_sum)
        return 0

    lax.fori_loop(0, NX, one_block, 0)


def values_kernel(where_ref, queries_ref, keys_ref, dout_ref, total_ref, out_ref, key_rows, sums):
    g, head, bound = where_ref[0], where_ref[1], where_ref[2]
    fill_keys(where_ref, keys_ref, key_rows)
    sums[...] = jnp.zeros_like(sums)

    def one_block(slot, _):
        block_start = (lax.rem(head - slot + NX, NX) * NG + g) * BLOCK
        query_rows = heads_as_rows(queries_ref[slot])
        dout_rows = heads_as_rows(dout_ref[slot])
        log_total = total_ref[slot]
        first, stop = chunk_range(block_start, bound)

        def one_chunk(chunk, _):
            chunk_start = pl.multiple_of(chunk * CHUNK, CHUNK)
            rows = pl.ds(chunk_start, CHUNK)
            scores = lax.dot_general(
                key_rows[rows, :],
                query_rows,
                (((1,), (1,)), ((), ())),
                preferred_element_type=jnp.float32,
            )
            whole = chunk_whole(chunk_start, block_start, bound)

            def add(weights):
                sums[rows, :] += jnp.dot(
                    weights.astype(jnp.bfloat16), dout_rows, preferred_element_type=jnp.float32
                )

            @pl.when(whole)
            def _():
                add(jnp.exp2(scores * exp2_scale - log_total))

            @pl.when(jnp.logical_not(whole))
            def _():
                visible = chunk_hidden(chunk_start, block_start, bound)
                add(jnp.where(visible, jnp.exp2(scores * exp2_scale - log_total), 0.0))

            return 0

        return lax.fori_loop(first, stop, one_chunk, 0)

    lax.fori_loop(0, NX, one_block, 0)
    for x in range(NX):
        for g_to in range(NG):
            out_ref[g_to, x] = sums[pl.ds((x * NG + g_to) * BLOCK, BLOCK), :].astype(out_ref.dtype)


def in_smem():
    return pl.BlockSpec(memory_space=pltpu.SMEM)


def in_vmem():
    return pl.BlockSpec(memory_space=pltpu.VMEM)


def attention_totals(where, queries, keys):
    return pl.pallas_call(
        totals_kernel,
        out_shape=jax.ShapeDtypeStruct((NX, 1, ROWS), jnp.float32),
        in_specs=[in_smem(), in_vmem(), in_vmem()],
        out_specs=in_vmem(),
        scratch_shapes=[
            pltpu.VMEM((SLAB, HD), jnp.bfloat16),
            pltpu.VMEM((CHUNK, ROWS), jnp.float32),
        ],
        compiler_params=pltpu.CompilerParams(vmem_limit_bytes=32 * 1024 * 1024),
        cost_estimate=pl.CostEstimate(
            flops=SLAB * SLAB * HD, bytes_accessed=2 << 20, transcendentals=SLAB * SLAB // 2
        ),
        name="attention_totals",
    )(where, queries, keys)


def attention_values(where, queries, keys, dout, totals):
    return pl.pallas_call(
        values_kernel,
        out_shape=jax.ShapeDtypeStruct((NG, NX, BLOCK, HD), jnp.bfloat16),
        in_specs=[in_smem(), in_vmem(), in_vmem(), in_vmem(), in_vmem()],
        out_specs=in_vmem(),
        scratch_shapes=[
            pltpu.VMEM((SLAB, HD), jnp.bfloat16),
            pltpu.VMEM((SLAB, HD), jnp.float32),
        ],
        compiler_params=pltpu.CompilerParams(vmem_limit_bytes=32 * 1024 * 1024),
        cost_estimate=pl.CostEstimate(
            flops=2 * SLAB * SLAB * HD, bytes_accessed=4 << 20, transcendentals=SLAB * SLAB // 2
        ),
        name="attention_values",
    )(where, queries, keys, dout, totals)


def decode_cached(dec_query, dec_key, cache_keys, cache_values, cache_len):
    step_count, row_total = dec_query.shape[:2]
    cache_rows = cache_keys.shape[1]
    score_scale = HD ** (-0.5)
    query_heads = dec_query.reshape(step_count, row_total, GROUP, HD)
    old_scores = (
        jnp.einsum("srgd,rcd->srgc", query_heads, cache_keys, preferred_element_type=jnp.float32)
        * score_scale
    )
    new_scores = (
        jnp.einsum("srgd,jrd->srgj", query_heads, dec_key, preferred_element_type=jnp.float32)
        * score_scale
    )
    old_visible = (jnp.arange(cache_rows, dtype=jnp.int32)[None, :] < cache_len[:, None])[
        None, :, None, :
    ]
    step_ids = jnp.arange(step_count, dtype=jnp.int32)
    new_visible = (step_ids[None, :] <= step_ids[:, None])[:, None, None, :]
    row_max = jnp.maximum(
        jnp.max(jnp.where(old_visible, old_scores, -jnp.inf), axis=3),
        jnp.max(jnp.where(new_visible, new_scores, -jnp.inf), axis=3),
    )[..., None]
    old_exp = jnp.where(old_visible, jnp.exp(old_scores - row_max), 0.0)
    new_exp = jnp.where(new_visible, jnp.exp(new_scores - row_max), 0.0)
    denom = jnp.sum(old_exp, axis=3, keepdims=True) + jnp.sum(new_exp, axis=3, keepdims=True)
    old_weights = (old_exp / denom).astype(jnp.bfloat16)
    new_weights = (new_exp / denom).astype(jnp.bfloat16)
    attended = jnp.einsum(
        "srgc,rcd->srgd", old_weights, cache_values, preferred_element_type=jnp.float32
    )
    return attended, new_weights


def sum_over_tp(value, core, bf=jnp.bfloat16):
    half = value.shape[1] // 2
    flip_core = lambda x, z, y, t: (x, z, y, t ^ 1)
    flip_chip = lambda x, z, y, t: (x, z, y, t ^ 2)
    mine = lax.dynamic_slice_in_dim(value, core * half, half, 1)
    other = lax.dynamic_slice_in_dim(value, (1 - core) * half, half, 1)
    on_chip = mine + route(other, flip_core)
    both = (on_chip + route(on_chip.astype(bf), flip_chip).astype(jnp.float32)).astype(bf)
    rest = route(both, flip_core)
    low = jnp.where(core == 0, both, rest)
    high = jnp.where(core == 0, rest, both)
    return jnp.concatenate([low, high], axis=1)


def shards(
    queries,
    attn_keys,
    hidden,
    out_grad,
    logp_new,
    logp_old,
    logp_ref,
    lengths,
    rewards,
    groups,
    master,
    first_moment,
    second_moment,
    dec_hidden,
    dec_query,
    dec_key,
    cache_keys,
    cache_values,
    cache_len,
    out_weight,
):
    bf, f32 = jnp.bfloat16, jnp.float32
    ctx = lax.axis_index("ctx")
    t = lax.axis_index("tp")
    x, g = ctx // NG, ctx % NG
    z, y = g // NY, g % NY

    def to_owner(r):
        return lambda x, z, y, s: (s + x + r, z, y, x + r)

    own_lengths = route(lengths, to_owner(0))[0]
    key_heads = attn_keys[0].reshape(BLOCK, KV, HD)
    query_heads = queries[0].reshape(BLOCK, KV, GROUP * HD)
    key_parts = jnp.stack(
        [route(pick(key_heads, (x + r) % KV, 1), to_owner(r)) for r in range(NX)]
    )
    query_parts = jnp.stack(
        [route(pick(query_heads, (x + r) % KV, 1), to_owner(r)) for r in range(NX)]
    )
    keys = lax.all_to_all(
        jnp.broadcast_to(key_parts[None], (NG, NX, BLOCK, HD)),
        "ctx",
        split_axis=0,
        concat_axis=0,
        axis_index_groups=[[a * NG + b for b in range(NG)] for a in range(NX)],
        tiled=True,
    )

    query_position = ctx * BLOCK + jnp.arange(BLOCK, dtype=jnp.int32)
    query_segment = segment_ids(lengths[0], query_position)
    own_advantage = pick(group_advantage(rewards, groups), t)
    token_weight = token_coef(
        own_advantage, query_segment, logp_new[0], logp_old[0], logp_ref[0], float(rewards.size)
    )
    dout_rows = (token_weight[:, None] * out_grad[0].astype(f32)).astype(bf)
    dout_heads = dout_rows.reshape(BLOCK, KV, GROUP * HD)
    dout_parts = jnp.stack(
        [route(pick(dout_heads, (x + r) % KV, 1), to_owner(r)) for r in range(NX)]
    )
    hidden_parts = [route(hidden[0], to_owner(r)) for r in range(NX)]

    state = jnp.stack([master, first_moment, second_moment]).reshape(3, 40, KV, HD)

    def over_tp(d):
        return lambda x, z, y, t: (x, z, y, t ^ d)

    moved = [pick(state, t, 2)] + [
        route(pick(state, t ^ d, 2), over_tp(d)) for d in range(1, NT)
    ]
    moved = jnp.stack(moved)
    by_row = jnp.stack([pick(moved, t ^ d) for d in range(NT)], axis=1)
    old_master, old_first, old_second = by_row.reshape(3, NT * 40, HD)

    cached, new_weights = decode_cached(dec_query, dec_key, cache_keys, cache_values, cache_len)

    where = jnp.stack([g, t, own_lengths[0]]).astype(jnp.int32)
    totals = attention_totals(where, query_parts, keys)
    partial = attention_values(where, query_parts, keys, dout_parts, totals)

    partial = partial.reshape(NZ, NY, NX, BLOCK, HD)

    def along_z(d):
        return lambda x, z, y, t: (x, z + d, y, t)

    over_z = pick(partial, z).astype(f32)
    for d in range(1, NZ):
        over_z = over_z + route(pick(partial, (z + d) % NZ), along_z(d)).astype(f32)
    flip_y = lambda x, z, y, t: (x, z, y + 1, t)
    dvalue = (pick(over_z, y) + route(pick(over_z, 1 - y), flip_y)).astype(bf)

    gradient = jnp.zeros((5120, HD), f32)
    for r in range(NX):
        gradient = gradient + lax.dot_general(
            hidden_parts[r],
            pick(dvalue, (t - r) % NX),
            (((0,), (0,)), ((), ())),
            preferred_element_type=f32,
        )
    terms = lax.all_to_all(
        gradient.astype(bf).reshape(NX * NG, NT * 40, HD),
        "ctx",
        split_axis=0,
        concat_axis=0,
        tiled=True,
    )
    gradient = jnp.sum(terms.astype(f32), axis=0)

    new_first = first_decay * old_first + (1.0 - first_decay) * gradient
    new_second = second_decay * old_second + (1.0 - second_decay) * gradient * gradient
    new_master = old_master - learn_rate * (
        new_first / (jnp.sqrt(new_second) + adam_eps) + decay_weight * old_master
    )
    rounded = new_master.astype(bf)
    rollout = lax.all_to_all(
        jnp.broadcast_to(rounded[None], (NX * NG, NT * 40, HD)),
        "ctx",
        split_axis=0,
        concat_axis=0,
        tiled=True,
    ).reshape(5120, HD)

    news = jnp.stack([new_master, new_first, new_second]).reshape(3, NT, 40, HD)
    back = [pick(news, t, 1)] + [
        route(pick(news, t ^ d, 1), over_tp(d)) for d in range(1, NT)
    ]
    back = jnp.stack(back)
    back = jnp.stack([pick(back, t ^ d) for d in range(NT)], axis=2)
    new_master, new_first, new_second = back.reshape(3, 40, KV * HD)

    step_count, dec_rows = dec_hidden.shape[:2]
    fresh = jnp.dot(
        dec_hidden.reshape(step_count * dec_rows, dec_hidden.shape[2]),
        rollout,
        preferred_element_type=f32,
    )
    fresh = fresh.reshape(step_count, dec_rows, HD).astype(bf).astype(f32)
    attended = cached
    for j in range(step_count):
        attended = attended + new_weights[..., j : j + 1].astype(f32) * fresh[j][None, :, None, :]
    attended = attended.astype(bf).reshape(step_count * dec_rows, GROUP * HD)
    partial_out = jnp.dot(attended, out_weight, preferred_element_type=f32)
    dec_out = sum_over_tp(partial_out, t % 2).reshape(step_count, dec_rows, out_weight.shape[1])
    return (new_master, new_first, new_second, rollout, dec_out)


def solution(mesh):
    return jax.shard_map(
        shards,
        mesh=mesh,
        in_specs=(
            P("tp", "ctx", None),
            P("tp", "ctx", None),
            P("tp", "ctx", None),
            P("tp", "ctx", None),
            P("tp", "ctx"),
            P("tp", "ctx"),
            P("tp", "ctx"),
            P("tp", None),
            P(),
            P(),
            P(("ctx", "tp"), None),
            P(("ctx", "tp"), None),
            P(("ctx", "tp"), None),
            P(None, "ctx", None),
            P(None, "ctx", "tp"),
            P(None, "ctx", "tp"),
            P("ctx", None, "tp"),
            P("ctx", None, "tp"),
            P("ctx"),
            P("tp", None),
        ),
        out_specs=(
            P(("ctx", "tp"), None),
            P(("ctx", "tp"), None),
            P(("ctx", "tp"), None),
            P(None, "tp"),
            P(None, "ctx", None),
        ),
        check_vma=False,
    )
```

```python
import math

import jax
import jax.numpy as jnp
from jax import lax
from jax.experimental import pallas as pl
from jax.experimental.pallas import tpu as pltpu
from jax.sharding import PartitionSpec as P

HD = 128
HEADS = 32
KV = 4
GROUP = HEADS // KV
BLOCK = 128
NX, NZ, NY, NT = 4, 4, 2, 4
NG = NZ * NY
SLAB = NX * NG * BLOCK
CHUNK = 512
ROWS = GROUP * BLOCK
LOWEST = -1e30

first_decay = 0.9
second_decay = 0.95
adam_eps = 1e-08
learn_rate = 0.001
decay_weight = 0.1
kl_weight = 0.1
exp2_scale = HD ** (-0.5) * math.log2(math.e)


def route(value, target):
    pairs = []
    for source in range(NX * NG * NT):
        ctx, t = divmod(source, NT)
        x, g = divmod(ctx, NG)
        z, y = divmod(g, NY)
        nx, nz, ny, nt = target(x, z, y, t)
        pairs.append((source, (((nx % NX) * NZ + nz % NZ) * NY + ny % NY) * NT + nt % NT))
    return lax.ppermute(value, ("ctx", "tp"), pairs)


def together(*values):
    return lax.optimization_barrier(values)


def pick(value, index, axis=0):
    return lax.dynamic_index_in_dim(value, index, axis, keepdims=False)


def segment_ids(lengths_row, position):
    doc_ends = jnp.cumsum(lengths_row)
    return jnp.sum((position[:, None] >= doc_ends[None, :]).astype(jnp.int32), axis=1)


def group_advantage(rewards, groups):
    flat_reward = rewards.reshape(-1)
    flat_group = groups.reshape(-1)
    same_group = (flat_group[:, None] == flat_group[None, :]).astype(jnp.float32)
    group_mean = jnp.sum(same_group * flat_reward[None, :], axis=1) / jnp.sum(same_group, axis=1)
    return (flat_reward - group_mean).reshape(rewards.shape)


def token_coef(own_advantage, segment, policy_logp, sample_logp, frozen_logp, divisor):
    labels = jnp.arange(own_advantage.shape[0], dtype=jnp.int32)
    picked = jnp.sum(
        jnp.where(segment[:, None] == labels[None, :], own_advantage[None, :], 0.0), axis=1
    )
    return (
        -jnp.exp(policy_logp - sample_logp) * picked
        + kl_weight * (1.0 - jnp.exp(frozen_logp - policy_logp))
    ) / divisor


def in_smem():
    return pl.BlockSpec(memory_space=pltpu.SMEM)


def in_vmem():
    return pl.BlockSpec(memory_space=pltpu.VMEM)


def attention_kernel(where_ref, *refs):
    block_refs, refs = refs[:NX], refs[NX:]
    keys_ref, out_ref, query_rows, dout_rows, scores, sums = refs
    g, bound, own = where_ref[0], where_ref[1], where_ref[2]
    for slot in range(NX):
        for h in range(GROUP):
            rows = pl.ds(h * BLOCK, BLOCK)
            query_rows[slot, rows, :] = block_refs[slot][:, pl.ds(h * HD, HD)]
            dout_rows[slot, rows, :] = block_refs[slot][:, pl.ds((GROUP + h) * HD, HD)]
    sums[...] = jnp.zeros_like(sums)

    def one_block(slot, _):
        block_start = (lax.rem(own - slot + NX, NX) * NG + g) * BLOCK
        latest_from = jnp.where(block_start + BLOCK - 1 >= bound, bound, 0)
        first = jnp.where(block_start >= bound, bound, 0) // CHUNK
        stop = (block_start + BLOCK - 1) // CHUNK + 1
        block_queries, block_douts = query_rows[slot], dout_rows[slot]

        def scored(chunk, row_max):
            start = pl.multiple_of(chunk * CHUNK, CHUNK)
            rows = pl.ds(start, CHUNK)
            scores[rows, :] = lax.dot_general(
                keys_ref[rows, :],
                block_queries,
                (((1,), (1,)), ((), ())),
                preferred_element_type=jnp.float32,
            )
            whole = (start + CHUNK - 1 <= block_start) & (start >= latest_from)

            @pl.when(jnp.logical_not(whole))
            def _():
                key_at = start + lax.broadcasted_iota(jnp.int32, (CHUNK, ROWS), 0)
                query_at = block_start + (
                    lax.broadcasted_iota(jnp.int32, (1, ROWS), 1) & (BLOCK - 1)
                )
                from_at = jnp.where(query_at >= bound, bound, 0)
                visible = (key_at <= query_at) & (key_at >= from_at)
                scores[rows, :] = jnp.where(visible, scores[rows, :], LOWEST)

            by_tile = scores[rows, :].reshape(CHUNK // 8, 8, ROWS)
            return jnp.maximum(row_max, jnp.max(by_tile, axis=0))

        row_max = lax.fori_loop(first, stop, scored, jnp.full((8, ROWS), LOWEST, jnp.float32))
        row_max = jnp.max(row_max, axis=0, keepdims=True) * exp2_scale

        def summed(chunk, row_sum):
            rows = pl.ds(pl.multiple_of(chunk * CHUNK, CHUNK), CHUNK)
            powers = jnp.exp2(scores[rows, :] * exp2_scale - row_max)
            scores[rows, :] = powers
            return row_sum + jnp.sum(powers.reshape(CHUNK // 8, 8, ROWS), axis=0)

        row_sum = lax.fori_loop(first, stop, summed, jnp.zeros((8, ROWS), jnp.float32))
        inverse = 1.0 / jnp.sum(row_sum, axis=0, keepdims=True)

        def added(chunk, _):
            rows = pl.ds(pl.multiple_of(chunk * CHUNK, CHUNK), CHUNK)
            sums[rows, :] += jnp.dot(
                (scores[rows, :] * inverse).astype(jnp.bfloat16),
                block_douts,
                preferred_element_type=jnp.float32,
            )
            return 0

        return lax.fori_loop(first, stop, added, 0)

    lax.fori_loop(0, NX, one_block, 0)
    for x in range(NX):
        for g_to in range(NG):
            out_ref[g_to, x] = sums[pl.ds((x * NG + g_to) * BLOCK, BLOCK), :].astype(out_ref.dtype)


def attention_terms(where, blocks, keys):
    return pl.pallas_call(
        attention_kernel,
        out_shape=jax.ShapeDtypeStruct((NG, NX, BLOCK, HD), jnp.bfloat16),
        in_specs=[in_smem()] + [in_vmem()] * (NX + 1),
        out_specs=in_vmem(),
        scratch_shapes=[
            pltpu.VMEM((NX, ROWS, HD), jnp.bfloat16),
            pltpu.VMEM((NX, ROWS, HD), jnp.bfloat16),
            pltpu.VMEM((SLAB, ROWS), jnp.float32),
            pltpu.VMEM((SLAB, HD), jnp.float32),
        ],
        compiler_params=pltpu.CompilerParams(vmem_limit_bytes=48 * 1024 * 1024),
        cost_estimate=pl.CostEstimate(
            flops=4 * SLAB * SLAB * HD, bytes_accessed=6 << 20, transcendentals=SLAB * SLAB // 2
        ),
        name="attention_terms",
    )(where, *blocks, keys)


def gradient_kernel(where_ref, dvalue_ref, h0_ref, h1_ref, h2_ref, h3_ref, out_ref):
    t = where_ref[3]
    hidden = jnp.concatenate([h0_ref[...], h1_ref[...], h2_ref[...], h3_ref[...]], axis=0)
    matching = jnp.concatenate([dvalue_ref[t ^ d].T for d in range(NX)], axis=1)
    by_column = jnp.dot(matching, hidden, preferred_element_type=jnp.float32)
    out_ref[...] = by_column.T.astype(out_ref.dtype)


def gradient_terms(where, dvalue, hidden_parts):
    width, tile = hidden_parts[0].shape[1], 1280
    columns = pl.BlockSpec((BLOCK, tile), lambda i: (0, i))
    return pl.pallas_call(
        gradient_kernel,
        grid=(width // tile,),
        out_shape=jax.ShapeDtypeStruct((width, HD), jnp.bfloat16),
        in_specs=[
            in_smem(),
            pl.BlockSpec((NX, BLOCK, HD), lambda i: (0, 0, 0)),
        ]
        + [columns] * NX,
        out_specs=pl.BlockSpec((tile, HD), lambda i: (i, 0)),
        cost_estimate=pl.CostEstimate(
            flops=2 * NX * BLOCK * width * HD, bytes_accessed=7 << 20, transcendentals=0
        ),
        name="gradient_terms",
    )(where, dvalue, *hidden_parts)


def decode_weights(dec_query, dec_key, cache_keys, cache_len):
    step_count, row_total = dec_query.shape[:2]
    cache_rows = cache_keys.shape[1]
    score_scale = HD ** (-0.5)
    query_heads = dec_query.reshape(step_count, row_total, GROUP, HD)
    old_scores = (
        jnp.einsum("srgd,rcd->srgc", query_heads, cache_keys, preferred_element_type=jnp.float32)
        * score_scale
    )
    new_scores = (
        jnp.einsum("srgd,jrd->srgj", query_heads, dec_key, preferred_element_type=jnp.float32)
        * score_scale
    )
    old_visible = (jnp.arange(cache_rows, dtype=jnp.int32)[None, :] < cache_len[:, None])[
        None, :, None, :
    ]
    step_ids = jnp.arange(step_count, dtype=jnp.int32)
    new_visible = (step_ids[None, :] <= step_ids[:, None])[:, None, None, :]
    row_max = jnp.maximum(
        jnp.max(jnp.where(old_visible, old_scores, -jnp.inf), axis=3),
        jnp.max(jnp.where(new_visible, new_scores, -jnp.inf), axis=3),
    )[..., None]
    old_exp = jnp.where(old_visible, jnp.exp(old_scores - row_max), 0.0)
    new_exp = jnp.where(new_visible, jnp.exp(new_scores - row_max), 0.0)
    denom = jnp.sum(old_exp, axis=3, keepdims=True) + jnp.sum(new_exp, axis=3, keepdims=True)
    old_weights = (old_exp / denom).astype(jnp.bfloat16)
    new_weights = (new_exp / denom).astype(jnp.bfloat16)
    return old_weights, new_weights


def decode_kernel(where_ref, hidden_ref, rollout_ref, cached_ref, weights_ref, out_weight_ref, out_ref, attended_ref):
    steps = weights_ref.shape[1] // GROUP
    rows = hidden_ref.shape[0] // steps

    @pl.when(pl.program_id(0) == 0)
    def _():
        fresh = jnp.dot(hidden_ref[...], rollout_ref[...], preferred_element_type=jnp.float32)
        fresh = fresh.astype(jnp.bfloat16).astype(jnp.float32)
        repeated = [
            jnp.concatenate([fresh[j * rows : (j + 1) * rows]] * steps, axis=0)
            for j in range(steps)
        ]
        for h in range(GROUP):
            columns = pl.ds(h * HD, HD)
            total = cached_ref[:, columns]
            for j in range(steps):
                at = h * steps + j
                total = total + weights_ref[:, at : at + 1] * repeated[j]
            attended_ref[:, columns] = total.astype(attended_ref.dtype)

    out_ref[...] = jnp.dot(
        attended_ref[...], out_weight_ref[...], preferred_element_type=jnp.float32
    )


def decode_outputs(where, dec_hidden, rollout, cached, weights, out_weight):
    rows, width = dec_hidden.shape
    tile = 640
    half_tiles = out_weight.shape[1] // tile // 2

    def whole(*shape):
        return pl.BlockSpec(shape, lambda i, where: (0, 0))

    return pl.pallas_call(
        decode_kernel,
        grid_spec=pltpu.PrefetchScalarGridSpec(
            num_scalar_prefetch=1,
            grid=(half_tiles,),
            in_specs=[
                whole(rows, width),
                whole(width, HD),
                whole(rows, GROUP * HD),
                whole(*weights.shape),
                pl.BlockSpec((GROUP * HD, tile), lambda i, where: (0, (1 - where[4]) * half_tiles + i)),
            ],
            out_specs=[
                pl.BlockSpec((rows, tile), lambda i, where: (0, i)),
                whole(rows, GROUP * HD),
            ],
        ),
        out_shape=[
            jax.ShapeDtypeStruct((rows, half_tiles * tile), jnp.float32),
            jax.ShapeDtypeStruct((rows, GROUP * HD), jnp.bfloat16),
        ],
        cost_estimate=pl.CostEstimate(
            flops=rows * width * HD * 2 + rows * GROUP * HD * 2560 * 2,
            bytes_accessed=9 << 20,
            transcendentals=0,
        ),
        compiler_params=pltpu.CompilerParams(vmem_limit_bytes=32 * 1024 * 1024),
        name="decode_outputs",
    )(where, dec_hidden, rollout, cached, weights, out_weight)


def own_kernel(where_ref, attended_ref, out_weight_ref, out_ref):
    out_ref[...] = jnp.dot(
        attended_ref[...], out_weight_ref[...], preferred_element_type=jnp.float32
    )


def own_outputs(where, attended, out_weight):
    rows, tile = attended.shape[0], 640
    half_tiles = out_weight.shape[1] // tile // 2
    return pl.pallas_call(
        own_kernel,
        grid_spec=pltpu.PrefetchScalarGridSpec(
            num_scalar_prefetch=1,
            grid=(half_tiles,),
            in_specs=[
                pl.BlockSpec((rows, GROUP * HD), lambda i, where: (0, 0)),
                pl.BlockSpec((GROUP * HD, tile), lambda i, where: (0, where[4] * half_tiles + i)),
            ],
            out_specs=pl.BlockSpec((rows, tile), lambda i, where: (0, i)),
        ),
        out_shape=jax.ShapeDtypeStruct((rows, half_tiles * tile), jnp.float32),
        cost_estimate=pl.CostEstimate(
            flops=rows * GROUP * HD * 2560 * 2, bytes_accessed=7 << 20, transcendentals=0
        ),
        name="own_outputs",
    )(where, attended, out_weight)


def join_kernel(where_ref, own_ref, rest_ref, out_ref):
    half = own_ref.shape[1]
    core = where_ref[4]
    out_ref[:, pl.ds(pl.multiple_of(core * half, half), half)] = own_ref[...]
    out_ref[:, pl.ds(pl.multiple_of((1 - core) * half, half), half)] = rest_ref[...]


def join_halves(where, own, rest):
    return pl.pallas_call(
        join_kernel,
        in_specs=[in_smem(), in_vmem(), in_vmem()],
        out_specs=in_vmem(),
        out_shape=jax.ShapeDtypeStruct((own.shape[0], 2 * own.shape[1]), own.dtype),
        name="join_halves",
    )(where, own, rest)


def shards(
    queries,
    attn_keys,
    hidden,
    out_grad,
    logp_new,
    logp_old,
    logp_ref,
    lengths,
    rewards,
    groups,
    master,
    first_moment,
    second_moment,
    dec_hidden,
    dec_query,
    dec_key,
    cache_keys,
    cache_values,
    cache_len,
    out_weight,
):
    bf, f32 = jnp.bfloat16, jnp.float32
    ctx = lax.axis_index("ctx")
    t = lax.axis_index("tp")
    x, g = ctx // NG, ctx % NG
    z, y = g // NY, g % NY

    def exchange(value, groups=None):
        return lax.all_to_all(
            value, "ctx", split_axis=0, concat_axis=0, axis_index_groups=groups, tiled=True
        )

    query_position = ctx * BLOCK + jnp.arange(BLOCK, dtype=jnp.int32)
    query_segment = segment_ids(lengths[0], query_position)
    own_advantage = pick(group_advantage(rewards, groups), t)
    token_weight = token_coef(
        own_advantage, query_segment, logp_new[0], logp_old[0], logp_ref[0], float(rewards.size)
    )
    dout_rows = (token_weight[:, None] * out_grad[0].astype(f32)).astype(bf)

    def along_x(d):
        return lambda x, z, y, t: (x + d, z, y, t)

    def for_head(head):
        width = GROUP * HD
        return jnp.concatenate(
            [
                lax.dynamic_slice_in_dim(queries[0], head * width, width, 1),
                lax.dynamic_slice_in_dim(dout_rows, head * width, width, 1),
            ],
            axis=1,
        )

    key_heads = attn_keys[0].reshape(BLOCK, KV, HD).transpose(1, 0, 2)
    key_heads = jnp.broadcast_to(key_heads[:, None], (NX, NG, BLOCK, HD))
    key_heads, *sent = together(key_heads, *[for_head((x + d) % NX) for d in range(NX)])
    blocks = [sent[0]] + [route(sent[d], along_x(d)) for d in range(1, NX)]
    keys = exchange(key_heads.reshape(NX * NG, BLOCK, HD)).reshape(SLAB, HD)

    def swap(x, z, y, t):
        return (t + 2 * (x // 2), z, y, x)

    def swap_and_flip(x, z, y, t):
        return (t + 2 * ((x ^ 2) // 2), z, y, x ^ 2)

    def flip_core(x, z, y, t):
        return (x, z, y, t ^ 1)

    def flip_chip(x, z, y, t):
        return (x, z, y, t ^ 2)

    state = jnp.stack([master, first_moment, second_moment]).reshape(3, 40, KV, HD)
    state, keys = together(state, keys)
    own_rows, keys, *blocks = together(hidden[0], keys, *blocks)
    hidden_parts = [route(own_rows, swap), None, route(own_rows, swap_and_flip), None]

    def over_tp(d):
        return lambda x, z, y, t: (x, z, y, t ^ d)

    moved = [pick(state, t, 2)] + [
        route(pick(state, t ^ d, 2), over_tp(d)) for d in range(1, NT)
    ]
    moved = jnp.stack(moved)
    by_row = jnp.stack([pick(moved, t ^ d) for d in range(NT)], axis=1)
    by_row = by_row.reshape(3, NT * 40, HD)

    old_weights, new_weights = decode_weights(dec_query, dec_key, cache_keys, cache_len)

    where = jnp.stack([g, lengths[0, 0], x, t, t % 2]).astype(jnp.int32)
    where, by_row, old_weights, new_weights = together(where, by_row, old_weights, new_weights)
    old_master, old_first, old_second = by_row
    partial = attention_terms(where, blocks, keys)

    along_zy = [[a * NG + b for b in range(NG)] for a in range(NX)]
    terms = exchange(partial.reshape(NG, NX * BLOCK, HD), along_zy)
    terms, hidden_parts[0], hidden_parts[2] = together(terms, hidden_parts[0], hidden_parts[2])
    dvalue = jnp.sum(terms.astype(f32), axis=0).astype(bf).reshape(NX, BLOCK, HD)
    dvalue = route(dvalue, swap)
    hidden_parts[1] = route(hidden_parts[0], flip_core)
    hidden_parts[3] = route(hidden_parts[2], flip_core)
    gradient = gradient_terms(where, dvalue, hidden_parts)
    terms = exchange(gradient.reshape(NX * NG, NT * 40, HD))
    gradient = jnp.sum(terms.astype(f32), axis=0)

    new_first = first_decay * old_first + (1.0 - first_decay) * gradient
    new_second = second_decay * old_second + (1.0 - second_decay) * gradient * gradient
    new_master = old_master - learn_rate * (
        new_first / (jnp.sqrt(new_second) + adam_eps) + decay_weight * old_master
    )
    cached = jnp.einsum(
        "srgc,rcd->srgd", old_weights, cache_values, preferred_element_type=f32
    ).reshape(-1, GROUP * HD)
    new_weights = new_weights.astype(f32).reshape(cached.shape[0], -1)
    rounded, cached, new_weights = together(new_master.astype(bf), cached, new_weights)
    rollout = exchange(jnp.broadcast_to(rounded[None], (NX * NG, NT * 40, HD))).reshape(5120, HD)

    news = jnp.stack([new_master, new_first, new_second]).reshape(3, NT, 40, HD)
    back = [pick(news, t, 1)] + [
        route(pick(news, t ^ d, 1), over_tp(d)) for d in range(1, NT)
    ]
    back = jnp.stack(back)
    back = jnp.stack([pick(back, t ^ d) for d in range(NT)], axis=2)
    rollout, back = together(rollout, back)
    new_master, new_first, new_second = back.reshape(3, 40, KV * HD)

    step_count, dec_rows = dec_hidden.shape[:2]
    rows = step_count * dec_rows
    other, attended = decode_outputs(
        where,
        dec_hidden.reshape(rows, dec_hidden.shape[2]),
        rollout,
        cached,
        new_weights,
        out_weight,
    )
    received = route(other, flip_core)
    on_chip = own_outputs(where, attended, out_weight) + received
    both = (on_chip + route(on_chip.astype(bf), flip_chip).astype(f32)).astype(bf)
    dec_out = join_halves(where, both, route(both, flip_core))
    dec_out = dec_out.reshape(step_count, dec_rows, out_weight.shape[1])
    return (new_master, new_first, new_second, rollout, dec_out)


def solution(mesh):
    return jax.shard_map(
        shards,
        mesh=mesh,
        in_specs=(
            P("tp", "ctx", None),
            P("tp", "ctx", None),
            P("tp", "ctx", None),
            P("tp", "ctx", None),
            P("tp", "ctx"),
            P("tp", "ctx"),
            P("tp", "ctx"),
            P("tp", None),
            P(),
            P(),
            P(("ctx", "tp"), None),
            P(("ctx", "tp"), None),
            P(("ctx", "tp"), None),
            P(None, "ctx", None),
            P(None, "ctx", "tp"),
            P(None, "ctx", "tp"),
            P("ctx", None, "tp"),
            P("ctx", None, "tp"),
            P("ctx"),
            P("tp", None),
        ),
        out_specs=(
            P(("ctx", "tp"), None),
            P(("ctx", "tp"), None),
            P(("ctx", "tp"), None),
            P(None, "tp"),
            P(None, "ctx", None),
        ),
        check_vma=False,
    )
```

```python
import math

import jax
import jax.numpy as jnp
from jax import lax
from jax.experimental import pallas as pl
from jax.experimental.pallas import tpu as pltpu
from jax.sharding import PartitionSpec as P

HD = 128
HEADS = 32
KV = 4
GROUP = HEADS // KV
BLOCK = 128
NX, NZ, NY, NT = 4, 4, 2, 4
NG = NZ * NY
SLAB = NX * NG * BLOCK
CHUNK = 512
ROWS = GROUP * BLOCK
LOWEST = -1e30

first_decay = 0.9
second_decay = 0.95
adam_eps = 1e-08
learn_rate = 0.001
decay_weight = 0.1
kl_weight = 0.1
exp2_scale = HD ** (-0.5) * math.log2(math.e)


def route(value, target):
    pairs = []
    for source in range(NX * NG * NT):
        ctx, t = divmod(source, NT)
        x, g = divmod(ctx, NG)
        z, y = divmod(g, NY)
        nx, nz, ny, nt = target(x, z, y, t)
        pairs.append((source, (((nx % NX) * NZ + nz % NZ) * NY + ny % NY) * NT + nt % NT))
    return lax.ppermute(value, ("ctx", "tp"), pairs)


def together(*values):
    return lax.optimization_barrier(values)


def pick(value, index, axis=0):
    return lax.dynamic_index_in_dim(value, index, axis, keepdims=False)


def segment_ids(lengths_row, position):
    doc_ends = jnp.cumsum(lengths_row)
    return jnp.sum((position[:, None] >= doc_ends[None, :]).astype(jnp.int32), axis=1)


def group_advantage(rewards, groups):
    flat_reward = rewards.reshape(-1)
    flat_group = groups.reshape(-1)
    same_group = (flat_group[:, None] == flat_group[None, :]).astype(jnp.float32)
    group_mean = jnp.sum(same_group * flat_reward[None, :], axis=1) / jnp.sum(same_group, axis=1)
    return (flat_reward - group_mean).reshape(rewards.shape)


def token_coef(own_advantage, segment, policy_logp, sample_logp, frozen_logp, divisor):
    labels = jnp.arange(own_advantage.shape[0], dtype=jnp.int32)
    picked = jnp.sum(
        jnp.where(segment[:, None] == labels[None, :], own_advantage[None, :], 0.0), axis=1
    )
    return (
        -jnp.exp(policy_logp - sample_logp) * picked
        + kl_weight * (1.0 - jnp.exp(frozen_logp - policy_logp))
    ) / divisor


def in_smem():
    return pl.BlockSpec(memory_space=pltpu.SMEM)


def in_vmem():
    return pl.BlockSpec(memory_space=pltpu.VMEM)


def attention_kernel(where_ref, *refs):
    block_refs, key_refs, refs = refs[:NX], refs[NX : NX + NG], refs[NX + NG :]
    out_ref, keys_ref, query_rows, dout_rows, scores, sums = refs
    g, bound, own = where_ref[0], where_ref[1], where_ref[2]
    for dz in range(NZ):
        for dy in range(NY):
            part = key_refs[dz * NY + dy]
            part_g = lax.rem(g // NY - dz + NZ, NZ) * NY + lax.rem(g - dy + NG, NY)
            for d in range(NX):
                part_x = lax.rem(own - d + NX, NX)
                rows = pl.ds(pl.multiple_of((part_x * NG + part_g) * BLOCK, BLOCK), BLOCK)
                keys_ref[rows, :] = part[d]
    for slot in range(NX):
        for h in range(GROUP):
            rows = pl.ds(h * BLOCK, BLOCK)
            query_rows[slot, rows, :] = block_refs[slot][:, pl.ds(h * HD, HD)]
            dout_rows[slot, rows, :] = block_refs[slot][:, pl.ds((GROUP + h) * HD, HD)]
    sums[...] = jnp.zeros_like(sums)

    def one_block(slot, _):
        block_start = (lax.rem(own - slot + NX, NX) * NG + g) * BLOCK
        latest_from = jnp.where(block_start + BLOCK - 1 >= bound, bound, 0)
        first = jnp.where(block_start >= bound, bound, 0) // CHUNK
        stop = (block_start + BLOCK - 1) // CHUNK + 1
        block_queries, block_douts = query_rows[slot], dout_rows[slot]

        def scored(chunk, row_max):
            start = pl.multiple_of(chunk * CHUNK, CHUNK)
            rows = pl.ds(start, CHUNK)
            scores[rows, :] = lax.dot_general(
                keys_ref[rows, :],
                block_queries,
                (((1,), (1,)), ((), ())),
                preferred_element_type=jnp.float32,
            )
            whole = (start + CHUNK - 1 <= block_start) & (start >= latest_from)

            @pl.when(jnp.logical_not(whole))
            def _():
                key_at = start + lax.broadcasted_iota(jnp.int32, (CHUNK, ROWS), 0)
                query_at = block_start + (
                    lax.broadcasted_iota(jnp.int32, (1, ROWS), 1) & (BLOCK - 1)
                )
                from_at = jnp.where(query_at >= bound, bound, 0)
                visible = (key_at <= query_at) & (key_at >= from_at)
                scores[rows, :] = jnp.where(visible, scores[rows, :], LOWEST)

            by_tile = scores[rows, :].reshape(CHUNK // 8, 8, ROWS)
            return jnp.maximum(row_max, jnp.max(by_tile, axis=0))

        row_max = lax.fori_loop(first, stop, scored, jnp.full((8, ROWS), LOWEST, jnp.float32))
        row_max = jnp.max(row_max, axis=0, keepdims=True) * exp2_scale

        def summed(chunk, row_sum):
            rows = pl.ds(pl.multiple_of(chunk * CHUNK, CHUNK), CHUNK)
            powers = jnp.exp2(scores[rows, :] * exp2_scale - row_max)
            scores[rows, :] = powers
            return row_sum + jnp.sum(powers.reshape(CHUNK // 8, 8, ROWS), axis=0)

        row_sum = lax.fori_loop(first, stop, summed, jnp.zeros((8, ROWS), jnp.float32))
        inverse = 1.0 / jnp.sum(row_sum, axis=0, keepdims=True)

        def added(chunk, _):
            rows = pl.ds(pl.multiple_of(chunk * CHUNK, CHUNK), CHUNK)
            sums[rows, :] += jnp.dot(
                (scores[rows, :] * inverse).astype(jnp.bfloat16),
                block_douts,
                preferred_element_type=jnp.float32,
            )
            return 0

        return lax.fori_loop(first, stop, added, 0)

    lax.fori_loop(0, NX, one_block, 0)
    for x in range(NX):
        for y in range(NY):
            for z in range(NZ):
                rows = pl.ds(((x * NZ + z) * NY + y) * BLOCK, BLOCK)
                out_ref[x * NY + y, z] = sums[rows, :].astype(out_ref.dtype)


def attention_terms(where, blocks, keys):
    return pl.pallas_call(
        attention_kernel,
        out_shape=jax.ShapeDtypeStruct((NX * NY, NZ, BLOCK, HD), jnp.bfloat16),
        in_specs=[in_smem()] + [in_vmem()] * (NX + NG),
        out_specs=in_vmem(),
        scratch_shapes=[
            pltpu.VMEM((SLAB, HD), jnp.bfloat16),
            pltpu.VMEM((NX, ROWS, HD), jnp.bfloat16),
            pltpu.VMEM((NX, ROWS, HD), jnp.bfloat16),
            pltpu.VMEM((SLAB, ROWS), jnp.float32),
            pltpu.VMEM((SLAB, HD), jnp.float32),
        ],
        compiler_params=pltpu.CompilerParams(vmem_limit_bytes=48 * 1024 * 1024),
        cost_estimate=pl.CostEstimate(
            flops=SLAB, bytes_accessed=SLAB, transcendentals=0
        ),
        name="attention_terms",
    )(where, *blocks, *keys)


def gradient_kernel(where_ref, dvalue_ref, h0_ref, h1_ref, h2_ref, h3_ref, out_ref):
    t = where_ref[3]
    hidden = jnp.concatenate([h0_ref[...], h1_ref[...], h2_ref[...], h3_ref[...]], axis=0)
    matching = jnp.concatenate([dvalue_ref[t ^ d].T for d in range(NX)], axis=1)
    by_column = jnp.dot(matching, hidden, preferred_element_type=jnp.float32)
    out_ref[...] = by_column.T.astype(out_ref.dtype)


def gradient_terms(where, dvalue, hidden_parts):
    width, tile = hidden_parts[0].shape[1], 1280
    columns = pl.BlockSpec((BLOCK, tile), lambda i: (0, i))
    return pl.pallas_call(
        gradient_kernel,
        grid=(width // tile,),
        out_shape=jax.ShapeDtypeStruct((width, HD), jnp.bfloat16),
        in_specs=[
            in_smem(),
            pl.BlockSpec((NX, BLOCK, HD), lambda i: (0, 0, 0)),
        ]
        + [columns] * NX,
        out_specs=pl.BlockSpec((tile, HD), lambda i: (i, 0)),
        cost_estimate=pl.CostEstimate(
            flops=2 * NX * BLOCK * width * HD, bytes_accessed=7 << 20, transcendentals=0
        ),
        name="gradient_terms",
    )(where, dvalue, *hidden_parts)


def decode_weights(dec_query, dec_key, cache_keys, cache_len):
    step_count, row_total = dec_query.shape[:2]
    cache_rows = cache_keys.shape[1]
    score_scale = HD ** (-0.5)
    query_heads = dec_query.reshape(step_count, row_total, GROUP, HD)
    old_scores = (
        jnp.einsum("srgd,rcd->srgc", query_heads, cache_keys, preferred_element_type=jnp.float32)
        * score_scale
    )
    new_scores = (
        jnp.einsum("srgd,jrd->srgj", query_heads, dec_key, preferred_element_type=jnp.float32)
        * score_scale
    )
    old_visible = (jnp.arange(cache_rows, dtype=jnp.int32)[None, :] < cache_len[:, None])[
        None, :, None, :
    ]
    step_ids = jnp.arange(step_count, dtype=jnp.int32)
    new_visible = (step_ids[None, :] <= step_ids[:, None])[:, None, None, :]
    row_max = jnp.maximum(
        jnp.max(jnp.where(old_visible, old_scores, -jnp.inf), axis=3),
        jnp.max(jnp.where(new_visible, new_scores, -jnp.inf), axis=3),
    )[..., None]
    old_exp = jnp.where(old_visible, jnp.exp(old_scores - row_max), 0.0)
    new_exp = jnp.where(new_visible, jnp.exp(new_scores - row_max), 0.0)
    denom = jnp.sum(old_exp, axis=3, keepdims=True) + jnp.sum(new_exp, axis=3, keepdims=True)
    old_weights = (old_exp / denom).astype(jnp.bfloat16)
    new_weights = (new_exp / denom).astype(jnp.bfloat16)
    return old_weights, new_weights


def shards(
    queries,
    attn_keys,
    hidden,
    out_grad,
    logp_new,
    logp_old,
    logp_ref,
    lengths,
    rewards,
    groups,
    master,
    first_moment,
    second_moment,
    dec_hidden,
    dec_query,
    dec_key,
    cache_keys,
    cache_values,
    cache_len,
    out_weight,
):
    bf, f32 = jnp.bfloat16, jnp.float32
    ctx = lax.axis_index("ctx")
    t = lax.axis_index("tp")
    x, g = ctx // NG, ctx % NG
    z, y = g // NY, g % NY

    def exchange(value, groups=None):
        return lax.all_to_all(
            value, "ctx", split_axis=0, concat_axis=0, axis_index_groups=groups, tiled=True
        )

    query_position = ctx * BLOCK + jnp.arange(BLOCK, dtype=jnp.int32)
    query_segment = segment_ids(lengths[0], query_position)
    own_advantage = pick(group_advantage(rewards, groups), t)
    token_weight = token_coef(
        own_advantage, query_segment, logp_new[0], logp_old[0], logp_ref[0], float(rewards.size)
    )
    dout_rows = (token_weight[:, None] * out_grad[0].astype(f32)).astype(bf)

    def along_x(d):
        return lambda x, z, y, t: (x + d, z, y, t)

    def for_head(head):
        width = GROUP * HD
        return jnp.concatenate(
            [
                lax.dynamic_slice_in_dim(queries[0], head * width, width, 1),
                lax.dynamic_slice_in_dim(dout_rows, head * width, width, 1),
            ],
            axis=1,
        )

    sent = [for_head((x + d) % NX) for d in range(NX)]
    blocks = [sent[0]] + [route(sent[d], along_x(d)) for d in range(1, NX)]

    def along_z(d):
        return lambda x, z, y, t: (x, z + d, y, t)

    def along_y(x, z, y, t):
        return (x, z, y + 1, t)

    key_heads = attn_keys[0].reshape(BLOCK, KV, HD)
    own_part = jnp.stack(
        [pick(key_heads, x, 1)]
        + [route(pick(key_heads, (x + d) % NX, 1), along_x(d)) for d in range(1, NX)]
    )
    z_parts = [own_part] + [route(own_part, along_z(d)) for d in range(1, NZ)]
    keys = [part for own in z_parts for part in (own, route(own, along_y))]

    def owner(x, z, y, s, head):
        return (x, s + 2 * (head // 2), y, head)

    def near(x, z, y, t):
        return owner(x, z, y, t, z ^ 1)

    def far(x, z, y, t):
        return owner(x, z, y, t, z ^ 3)

    def swap(x, z, y, t):
        return owner(z, z, y, t, x)

    def flip_core(x, z, y, t):
        return (x, z, y, t ^ 1)

    def flip_chip(x, z, y, t):
        return (x, z, y, t ^ 2)

    state = jnp.stack([master, first_moment, second_moment]).reshape(3, 40, KV, HD)
    own_rows = hidden[0]
    hidden_parts = [None, route(own_rows, near), None, route(own_rows, far)]

    def over_tp(d):
        return lambda x, z, y, t: (x, z, y, t ^ d)

    moved = [pick(state, t, 2)] + [
        route(pick(state, t ^ d, 2), over_tp(d)) for d in range(1, NT)
    ]
    moved = jnp.stack(moved)
    by_row = jnp.stack([pick(moved, t ^ d) for d in range(NT)], axis=1)
    by_row = by_row.reshape(3, NT * 40, HD)

    old_weights, new_weights = decode_weights(dec_query, dec_key, cache_keys, cache_len)

    where = jnp.stack([g, lengths[0, 0], x, t]).astype(jnp.int32)
    where, by_row, old_weights, new_weights = together(where, by_row, old_weights, new_weights)
    old_master, old_first, old_second = by_row
    partial = attention_terms(where, blocks, keys)

    along_zy = [[a * NG + b for b in range(NG)] for a in range(NX)]
    terms = exchange(partial.reshape(NG, NZ * BLOCK, HD), along_zy)
    terms, hidden_parts[1], hidden_parts[3] = together(terms, hidden_parts[1], hidden_parts[3])
    dvalue = jnp.sum(terms.astype(f32), axis=0).astype(bf).reshape(NZ, BLOCK, HD)
    dvalue = route(dvalue, swap)
    hidden_parts[0] = route(hidden_parts[1], flip_core)
    hidden_parts[2] = route(hidden_parts[3], flip_core)
    gradient = gradient_terms(where, dvalue, hidden_parts)
    terms = exchange(gradient.reshape(NX * NG, NT * 40, HD))
    gradient = jnp.sum(terms.astype(f32), axis=0)

    new_first = first_decay * old_first + (1.0 - first_decay) * gradient
    new_second = second_decay * old_second + (1.0 - second_decay) * gradient * gradient
    new_master = old_master - learn_rate * (
        new_first / (jnp.sqrt(new_second) + adam_eps) + decay_weight * old_master
    )
    cached = jnp.einsum(
        "srgc,rcd->srgd", old_weights, cache_values, preferred_element_type=f32
    )
    core, half = t % 2, out_weight.shape[1] // 2
    own_weight = lax.dynamic_slice_in_dim(out_weight, core * half, half, 1)
    other_weight = lax.dynamic_slice_in_dim(out_weight, (1 - core) * half, half, 1)
    rounded, cached, own_weight, other_weight = together(
        new_master.astype(bf), cached, own_weight, other_weight
    )
    rollout = exchange(jnp.broadcast_to(rounded[None], (NX * NG, NT * 40, HD))).reshape(5120, HD)

    news = jnp.stack([new_master, new_first, new_second]).reshape(3, NT, 40, HD)
    back = [pick(news, t, 1)] + [
        route(pick(news, t ^ d, 1), over_tp(d)) for d in range(1, NT)
    ]
    back = jnp.stack(back)
    back = jnp.stack([pick(back, t ^ d) for d in range(NT)], axis=2)
    rollout, back = together(rollout, back)
    new_master, new_first, new_second = back.reshape(3, 40, KV * HD)

    step_count, dec_rows = dec_hidden.shape[:2]
    rows = step_count * dec_rows
    fresh = jnp.dot(
        dec_hidden.reshape(rows, dec_hidden.shape[2]), rollout, preferred_element_type=f32
    )
    fresh = fresh.reshape(step_count, dec_rows, HD).astype(bf).astype(f32)
    attended = cached
    for j in range(step_count):
        attended = attended + new_weights[..., j : j + 1].astype(f32) * fresh[j][None, :, None, :]
    attended = attended.astype(bf).reshape(rows, GROUP * HD)

    received = route(jnp.dot(attended, other_weight, preferred_element_type=f32), flip_core)
    (own_out,) = together(jnp.dot(attended, own_weight, preferred_element_type=f32))
    on_chip = own_out + received
    both = (on_chip + route(on_chip.astype(bf), flip_chip).astype(f32)).astype(bf)
    rest = route(both, flip_core)
    dec_out = jnp.zeros((rows, 2 * half), bf)
    dec_out = lax.dynamic_update_slice_in_dim(dec_out, both, core * half, 1)
    dec_out = lax.dynamic_update_slice_in_dim(dec_out, rest, (1 - core) * half, 1)
    dec_out = dec_out.reshape(step_count, dec_rows, 2 * half)
    return (new_master, new_first, new_second, rollout, dec_out)


def solution(mesh):
    return jax.shard_map(
        shards,
        mesh=mesh,
        in_specs=(
            P("tp", "ctx", None),
            P("tp", "ctx", None),
            P("tp", "ctx", None),
            P("tp", "ctx", None),
            P("tp", "ctx"),
            P("tp", "ctx"),
            P("tp", "ctx"),
            P("tp", None),
            P(),
            P(),
            P(("ctx", "tp"), None),
            P(("ctx", "tp"), None),
            P(("ctx", "tp"), None),
            P(None, "ctx", None),
            P(None, "ctx", "tp"),
            P(None, "ctx", "tp"),
            P("ctx", None, "tp"),
            P("ctx", None, "tp"),
            P("ctx"),
            P("tp", None),
        ),
        out_specs=(
            P(("ctx", "tp"), None),
            P(("ctx", "tp"), None),
            P(("ctx", "tp"), None),
            P(None, "tp"),
            P(None, "ctx", None),
        ),
        check_vma=False,
    )
```

```python
import math

import jax
import jax.numpy as jnp
from jax import lax
from jax.experimental import pallas as pl
from jax.experimental.pallas import tpu as pltpu
from jax.sharding import PartitionSpec as P

HD = 128
HEADS = 32
KV = 4
GROUP = HEADS // KV
BLOCK = 128
NX, NZ, NY, NT = 4, 4, 2, 4
NG = NZ * NY
SLAB = NX * NG * BLOCK
CHUNK = 512
ROWS = GROUP * BLOCK
LOWEST = -1e30

first_decay = 0.9
second_decay = 0.95
adam_eps = 1e-08
learn_rate = 0.001
decay_weight = 0.1
kl_weight = 0.1
exp2_scale = HD ** (-0.5) * math.log2(math.e)


def route(value, target):
    pairs = []
    for source in range(NX * NG * NT):
        ctx, t = divmod(source, NT)
        x, g = divmod(ctx, NG)
        z, y = divmod(g, NY)
        nx, nz, ny, nt = target(x, z, y, t)
        pairs.append((source, (((nx % NX) * NZ + nz % NZ) * NY + ny % NY) * NT + nt % NT))
    return lax.ppermute(value, ("ctx", "tp"), pairs)


def together(*values):
    return lax.optimization_barrier(values)


def pick(value, index, axis=0):
    return lax.dynamic_index_in_dim(value, index, axis, keepdims=False)


def segment_ids(lengths_row, position):
    doc_ends = jnp.cumsum(lengths_row)
    return jnp.sum((position[:, None] >= doc_ends[None, :]).astype(jnp.int32), axis=1)


def group_advantage(rewards, groups):
    flat_reward = rewards.reshape(-1)
    flat_group = groups.reshape(-1)
    same_group = (flat_group[:, None] == flat_group[None, :]).astype(jnp.float32)
    group_mean = jnp.sum(same_group * flat_reward[None, :], axis=1) / jnp.sum(same_group, axis=1)
    return (flat_reward - group_mean).reshape(rewards.shape)


def token_coef(own_advantage, segment, policy_logp, sample_logp, frozen_logp, divisor):
    labels = jnp.arange(own_advantage.shape[0], dtype=jnp.int32)
    picked = jnp.sum(
        jnp.where(segment[:, None] == labels[None, :], own_advantage[None, :], 0.0), axis=1
    )
    return (
        -jnp.exp(policy_logp - sample_logp) * picked
        + kl_weight * (1.0 - jnp.exp(frozen_logp - policy_logp))
    ) / divisor


def in_smem():
    return pl.BlockSpec(memory_space=pltpu.SMEM)


def in_vmem():
    return pl.BlockSpec(memory_space=pltpu.VMEM)


def attention_kernel(where_ref, *refs):
    block_refs, key_refs, refs = refs[:NX], refs[NX : NX + NG], refs[NX + NG :]
    out_ref, keys_ref, query_columns, dout_rows, scores, sums, powers_sum = refs
    g, bound, own = where_ref[0], where_ref[1], where_ref[2]
    for dz in range(NZ):
        for dy in range(NY):
            part = key_refs[dz * NY + dy]
            part_g = lax.rem(g // NY - dz + NZ, NZ) * NY + lax.rem(g - dy + NG, NY)
            for d in range(NX):
                part_x = lax.rem(own - d + NX, NX)
                rows = pl.ds(pl.multiple_of((part_x * NG + part_g) * BLOCK, BLOCK), BLOCK)
                keys_ref[rows, :] = part[d]
    for slot in range(NX):
        for h in range(GROUP):
            rows = pl.ds(h * BLOCK, BLOCK)
            query_columns[slot, :, rows] = block_refs[slot][:, pl.ds(h * HD, HD)].T
            dout_rows[slot, rows, :] = block_refs[slot][:, pl.ds((GROUP + h) * HD, HD)]
    sums[...] = jnp.zeros_like(sums)

    def key_norm(i, longest):
        rows = pl.ds(pl.multiple_of(i * CHUNK, CHUNK), CHUNK)
        block = keys_ref[rows, :].astype(jnp.float32)
        norms = jnp.sum(block * block, axis=1, keepdims=True)
        return jnp.maximum(longest, jnp.max(norms, axis=0, keepdims=True))

    longest_key = lax.fori_loop(0, SLAB // CHUNK, key_norm, jnp.zeros((1, 1), jnp.float32))

    def one_block(slot, _):
        block_start = (lax.rem(own - slot + NX, NX) * NG + g) * BLOCK
        latest_from = jnp.where(block_start + BLOCK - 1 >= bound, bound, 0)
        first = jnp.where(block_start >= bound, bound, 0) // CHUNK
        stop = (block_start + BLOCK - 1) // CHUNK + 1
        block_queries, block_douts = query_columns[slot], dout_rows[slot]

        def scored(rows):
            return jnp.dot(keys_ref[rows, :], block_queries, preferred_element_type=jnp.float32)

        def is_visible(start):
            key_at = start + lax.broadcasted_iota(jnp.int32, (CHUNK, ROWS), 0)
            query_at = block_start + (lax.broadcasted_iota(jnp.int32, (1, ROWS), 1) & (BLOCK - 1))
            from_at = jnp.where(query_at >= bound, bound, 0)
            return (key_at <= query_at) & (key_at >= from_at)

        def by_tile(value):
            return value.reshape(CHUNK // 8, 8, ROWS)

        def add_powers(rows, powers):
            scores[rows, :] = powers
            powers_sum[...] += jnp.sum(by_tile(powers), axis=0)

        as_float = block_queries.astype(jnp.float32)
        norms = jnp.sum(as_float * as_float, axis=0, keepdims=True)
        limit = jnp.sqrt(norms * longest_key) * (1.001 * exp2_scale)
        powers_sum[...] = jnp.zeros_like(powers_sum)

        def from_limit(chunk, _):
            start = pl.multiple_of(chunk * CHUNK, CHUNK)
            rows = pl.ds(start, CHUNK)
            whole = (start + CHUNK - 1 <= block_start) & (start >= latest_from)

            @pl.when(whole)
            def _():
                add_powers(rows, jnp.exp2(scored(rows) * exp2_scale - limit))

            @pl.when(jnp.logical_not(whole))
            def _():
                powers = jnp.exp2(scored(rows) * exp2_scale - limit)
                add_powers(rows, jnp.where(is_visible(start), powers, 0.0))

            return 0

        lax.fori_loop(first, stop, from_limit, 0)

        total = jnp.sum(powers_sum[...], axis=0, keepdims=True)
        kept = jnp.min(jnp.where(total >= 2.0**-60, 1.0, 0.0))

        @pl.when(kept < 0.5)
        def _():
            def masked(chunk, row_max):
                start = pl.multiple_of(chunk * CHUNK, CHUNK)
                rows = pl.ds(start, CHUNK)
                scores[rows, :] = jnp.where(is_visible(start), scored(rows), LOWEST)
                return jnp.maximum(row_max, jnp.max(by_tile(scores[rows, :]), axis=0))

            row_max = lax.fori_loop(first, stop, masked, jnp.full((8, ROWS), LOWEST, jnp.float32))
            row_max = jnp.max(row_max, axis=0, keepdims=True) * exp2_scale
            powers_sum[...] = jnp.zeros_like(powers_sum)

            def from_maximum(chunk, _):
                rows = pl.ds(pl.multiple_of(chunk * CHUNK, CHUNK), CHUNK)
                add_powers(rows, jnp.exp2(scores[rows, :] * exp2_scale - row_max))
                return 0

            lax.fori_loop(first, stop, from_maximum, 0)

        inverse = 1.0 / jnp.sum(powers_sum[...], axis=0, keepdims=True)

        def added(chunk, _):
            rows = pl.ds(pl.multiple_of(chunk * CHUNK, CHUNK), CHUNK)
            sums[rows, :] += jnp.dot(
                (scores[rows, :] * inverse).astype(jnp.bfloat16),
                block_douts,
                preferred_element_type=jnp.float32,
            )
            return 0

        return lax.fori_loop(first, stop, added, 0)

    lax.fori_loop(0, NX, one_block, 0)
    for x in range(NX):
        for y in range(NY):
            for z in range(NZ):
                rows = pl.ds(((x * NZ + z) * NY + y) * BLOCK, BLOCK)
                out_ref[x * NY + y, z] = sums[rows, :].astype(out_ref.dtype)


def attention_terms(where, blocks, keys):
    return pl.pallas_call(
        attention_kernel,
        out_shape=jax.ShapeDtypeStruct((NX * NY, NZ, BLOCK, HD), jnp.bfloat16),
        in_specs=[in_smem()] + [in_vmem()] * (NX + NG),
        out_specs=in_vmem(),
        scratch_shapes=[
            pltpu.VMEM((SLAB, HD), jnp.bfloat16),
            pltpu.VMEM((NX, HD, ROWS), jnp.bfloat16),
            pltpu.VMEM((NX, ROWS, HD), jnp.bfloat16),
            pltpu.VMEM((SLAB, ROWS), jnp.float32),
            pltpu.VMEM((SLAB, HD), jnp.float32),
            pltpu.VMEM((8, ROWS), jnp.float32),
        ],
        compiler_params=pltpu.CompilerParams(vmem_limit_bytes=48 * 1024 * 1024),
        cost_estimate=pl.CostEstimate(
            flops=SLAB, bytes_accessed=SLAB, transcendentals=0
        ),
        name="attention_terms",
    )(where, *blocks, *keys)


def gradient_kernel(where_ref, dvalue_ref, h0_ref, h1_ref, h2_ref, h3_ref, out_ref):
    t = where_ref[3]
    hidden = jnp.concatenate([h0_ref[...], h1_ref[...], h2_ref[...], h3_ref[...]], axis=0)
    matching = jnp.concatenate([dvalue_ref[t ^ d].T for d in range(NX)], axis=1)
    by_column = jnp.dot(matching, hidden, preferred_element_type=jnp.float32)
    out_ref[...] = by_column.T.astype(out_ref.dtype)


def gradient_terms(where, dvalue, hidden_parts):
    width, tile = hidden_parts[0].shape[1], 1280
    columns = pl.BlockSpec((BLOCK, tile), lambda i: (0, i))
    return pl.pallas_call(
        gradient_kernel,
        grid=(width // tile,),
        out_shape=jax.ShapeDtypeStruct((width, HD), jnp.bfloat16),
        in_specs=[
            in_smem(),
            pl.BlockSpec((NX, BLOCK, HD), lambda i: (0, 0, 0)),
        ]
        + [columns] * NX,
        out_specs=pl.BlockSpec((tile, HD), lambda i: (i, 0)),
        cost_estimate=pl.CostEstimate(
            flops=2 * NX * BLOCK * width * HD, bytes_accessed=7 << 20, transcendentals=0
        ),
        name="gradient_terms",
    )(where, dvalue, *hidden_parts)


def copy_kernel(from_ref, to_ref):
    to_ref[...] = from_ref[...]


def copied(value):
    tile = pl.BlockSpec((value.shape[0] // 4, value.shape[1]), lambda i: (i, 0))
    return pl.pallas_call(
        copy_kernel,
        grid=(4,),
        in_specs=[tile],
        out_specs=tile,
        out_shape=jax.ShapeDtypeStruct(value.shape, value.dtype),
        cost_estimate=pl.CostEstimate(
            flops=0, bytes_accessed=4 * value.size, transcendentals=0
        ),
        name="copied",
    )(value)


def decode_weights(dec_query, dec_key, cache_keys, cache_len):
    step_count, row_total = dec_query.shape[:2]
    cache_rows = cache_keys.shape[1]
    score_scale = HD ** (-0.5)
    query_heads = dec_query.reshape(step_count, row_total, GROUP, HD)
    old_scores = (
        jnp.einsum("srgd,rcd->srgc", query_heads, cache_keys, preferred_element_type=jnp.float32)
        * score_scale
    )
    new_scores = (
        jnp.einsum("srgd,jrd->srgj", query_heads, dec_key, preferred_element_type=jnp.float32)
        * score_scale
    )
    old_visible = (jnp.arange(cache_rows, dtype=jnp.int32)[None, :] < cache_len[:, None])[
        None, :, None, :
    ]
    step_ids = jnp.arange(step_count, dtype=jnp.int32)
    new_visible = (step_ids[None, :] <= step_ids[:, None])[:, None, None, :]
    row_max = jnp.maximum(
        jnp.max(jnp.where(old_visible, old_scores, -jnp.inf), axis=3),
        jnp.max(jnp.where(new_visible, new_scores, -jnp.inf), axis=3),
    )[..., None]
    old_exp = jnp.where(old_visible, jnp.exp(old_scores - row_max), 0.0)
    new_exp = jnp.where(new_visible, jnp.exp(new_scores - row_max), 0.0)
    denom = jnp.sum(old_exp, axis=3, keepdims=True) + jnp.sum(new_exp, axis=3, keepdims=True)
    old_weights = (old_exp / denom).astype(jnp.bfloat16)
    new_weights = (new_exp / denom).astype(jnp.bfloat16)
    return old_weights, new_weights


def shards(
    queries,
    attn_keys,
    hidden,
    out_grad,
    logp_new,
    logp_old,
    logp_ref,
    lengths,
    rewards,
    groups,
    master,
    first_moment,
    second_moment,
    dec_hidden,
    dec_query,
    dec_key,
    cache_keys,
    cache_values,
    cache_len,
    out_weight,
):
    bf, f32 = jnp.bfloat16, jnp.float32
    ctx = lax.axis_index("ctx")
    t = lax.axis_index("tp")
    x, g = ctx // NG, ctx % NG
    z, y = g // NY, g % NY

    def exchange(value, groups=None):
        return lax.all_to_all(
            value, "ctx", split_axis=0, concat_axis=0, axis_index_groups=groups, tiled=True
        )

    query_position = ctx * BLOCK + jnp.arange(BLOCK, dtype=jnp.int32)
    query_segment = segment_ids(lengths[0], query_position)
    own_advantage = pick(group_advantage(rewards, groups), t)
    token_weight = token_coef(
        own_advantage, query_segment, logp_new[0], logp_old[0], logp_ref[0], float(rewards.size)
    )
    dout_rows = (token_weight[:, None] * out_grad[0].astype(f32)).astype(bf)

    def along_x(d):
        return lambda x, z, y, t: (x + d, z, y, t)

    def for_head(head):
        width = GROUP * HD
        return jnp.concatenate(
            [
                lax.dynamic_slice_in_dim(queries[0], head * width, width, 1),
                lax.dynamic_slice_in_dim(dout_rows, head * width, width, 1),
            ],
            axis=1,
        )

    sent = [for_head((x + d) % NX) for d in range(NX)]
    def along_z(d):
        return lambda x, z, y, t: (x, z + d, y, t)

    def along_y(x, z, y, t):
        return (x, z, y + 1, t)

    key_heads = attn_keys[0].reshape(BLOCK, KV, HD)
    own_part = jnp.stack(
        [pick(key_heads, x, 1)]
        + [route(pick(key_heads, (x + d) % NX, 1), along_x(d)) for d in range(1, NX)]
    )
    blocks = [sent[0]] + [route(sent[d], along_x(d)) for d in range(1, NX)]
    z_parts = [own_part] + [route(own_part, along_z(d)) for d in range(1, NZ)]
    keys = [part for own in z_parts for part in (own, route(own, along_y))]

    def owner(x, z, y, s, head):
        return (x, s + 2 * (head // 2), y, head)

    def near(x, z, y, t):
        return owner(x, z, y, t, z ^ 1)

    def far(x, z, y, t):
        return owner(x, z, y, t, z ^ 3)

    def swap(x, z, y, t):
        return owner(z, z, y, t, x)

    def flip_core(x, z, y, t):
        return (x, z, y, t ^ 1)

    def flip_chip(x, z, y, t):
        return (x, z, y, t ^ 2)

    own_rows = hidden[0]
    hidden_parts = [None, route(own_rows, near), None, route(own_rows, far)]

    where = jnp.stack([g, lengths[0, 0], x, t]).astype(jnp.int32)
    partial = attention_terms(where, blocks, keys)
    partial, dec_query, *state = together(partial, dec_query, master, first_moment, second_moment)

    state = jnp.stack(state).reshape(3, 40, KV, HD)

    def over_tp(d):
        return lambda x, z, y, t: (x, z, y, t ^ d)

    moved = [pick(state, t, 2)] + [
        route(pick(state, t ^ d, 2), over_tp(d)) for d in range(1, NT)
    ]
    moved = jnp.stack(moved)
    by_row = jnp.stack([pick(moved, t ^ d) for d in range(NT)], axis=1)
    by_row = by_row.reshape(3, NT * 40, HD)

    old_weights, new_weights = decode_weights(dec_query, dec_key, cache_keys, cache_len)

    along_zy = [[a * NG + b for b in range(NG)] for a in range(NX)]
    terms = exchange(partial.reshape(NG, NZ * BLOCK, HD), along_zy)
    terms, hidden_parts[1], hidden_parts[3], by_row, old_weights, new_weights = together(
        terms, hidden_parts[1], hidden_parts[3], by_row, old_weights, new_weights
    )
    old_master, old_first, old_second = by_row
    dvalue = jnp.sum(terms.astype(f32), axis=0).astype(bf).reshape(NZ, BLOCK, HD)
    dvalue = route(dvalue, swap)
    hidden_parts[0] = route(hidden_parts[1], flip_core)
    hidden_parts[2] = route(hidden_parts[3], flip_core)
    gradient = gradient_terms(where, dvalue, hidden_parts)
    gradient, out_weight, old_weights = together(gradient, out_weight, old_weights)
    terms = exchange(gradient.reshape(NX * NG, NT * 40, HD))
    gradient = jnp.sum(terms.astype(f32), axis=0)

    new_first = first_decay * old_first + (1.0 - first_decay) * gradient
    new_second = second_decay * old_second + (1.0 - second_decay) * gradient * gradient
    new_master = old_master - learn_rate * (
        new_first / (jnp.sqrt(new_second) + adam_eps) + decay_weight * old_master
    )
    cached = jnp.einsum(
        "srgc,rcd->srgd", old_weights, cache_values, preferred_element_type=f32
    )
    core, half = t % 2, out_weight.shape[1] // 2
    own_weight = lax.dynamic_slice_in_dim(out_weight, core * half, half, 1)
    other_weight = lax.dynamic_slice_in_dim(out_weight, (1 - core) * half, half, 1)
    rounded, cached, own_weight, other_weight = together(
        new_master.astype(bf), cached, own_weight, other_weight
    )
    rollout = exchange(jnp.broadcast_to(rounded[None], (NX * NG, NT * 40, HD))).reshape(5120, HD)

    news = jnp.stack([new_master, new_first, new_second]).reshape(3, NT, 40, HD)
    back = [pick(news, t, 1)] + [
        route(pick(news, t ^ d, 1), over_tp(d)) for d in range(1, NT)
    ]
    back = jnp.stack(back)
    back = jnp.stack([pick(back, t ^ d) for d in range(NT)], axis=2)
    rollout, back = together(rollout, back)
    new_master, new_first, new_second = back.reshape(3, 40, KV * HD)

    step_count, dec_rows = dec_hidden.shape[:2]
    rows = step_count * dec_rows
    fresh = jnp.dot(
        dec_hidden.reshape(rows, dec_hidden.shape[2]), rollout, preferred_element_type=f32
    )
    fresh = fresh.reshape(step_count, dec_rows, HD).astype(bf).astype(f32)
    attended = cached
    for j in range(step_count):
        attended = attended + new_weights[..., j : j + 1].astype(f32) * fresh[j][None, :, None, :]
    attended = attended.astype(bf).reshape(rows, GROUP * HD)

    received = route(jnp.dot(attended, other_weight, preferred_element_type=f32), flip_core)
    (own_out,) = together(jnp.dot(attended, own_weight, preferred_element_type=f32))
    on_chip = own_out + received
    from_chip, rollout = together(route(on_chip.astype(bf), flip_chip), copied(rollout))
    both = (on_chip + from_chip.astype(f32)).astype(bf)
    rest = route(both, flip_core)
    dec_out = jnp.zeros((rows, 2 * half), bf)
    dec_out = lax.dynamic_update_slice_in_dim(dec_out, both, core * half, 1)
    dec_out = lax.dynamic_update_slice_in_dim(dec_out, rest, (1 - core) * half, 1)
    dec_out = dec_out.reshape(step_count, dec_rows, 2 * half)
    return (new_master, new_first, new_second, rollout, dec_out)


def solution(mesh):
    return jax.shard_map(
        shards,
        mesh=mesh,
        in_specs=(
            P("tp", "ctx", None),
            P("tp", "ctx", None),
            P("tp", "ctx", None),
            P("tp", "ctx", None),
            P("tp", "ctx"),
            P("tp", "ctx"),
            P("tp", "ctx"),
            P("tp", None),
            P(),
            P(),
            P(("ctx", "tp"), None),
            P(("ctx", "tp"), None),
            P(("ctx", "tp"), None),
            P(None, "ctx", None),
            P(None, "ctx", "tp"),
            P(None, "ctx", "tp"),
            P("ctx", None, "tp"),
            P("ctx", None, "tp"),
            P("ctx"),
            P("tp", None),
        ),
        out_specs=(
            P(("ctx", "tp"), None),
            P(("ctx", "tp"), None),
            P(("ctx", "tp"), None),
            P(None, "tp"),
            P(None, "ctx", None),
        ),
        check_vma=False,
    )
```

```python
import math

import jax
import jax.numpy as jnp
from jax import lax
from jax.experimental import pallas as pl
from jax.experimental.pallas import tpu as pltpu
from jax.sharding import PartitionSpec as P

HD = 128
HEADS = 32
KV = 4
GROUP = HEADS // KV
BLOCK = 128
NX, NZ, NY, NT = 4, 4, 2, 4
NG = NZ * NY
SLAB = NX * NG * BLOCK
CHUNK = 512
ROWS = GROUP * BLOCK
LOWEST = -1e30

first_decay = 0.9
second_decay = 0.95
adam_eps = 1e-08
learn_rate = 0.001
decay_weight = 0.1
kl_weight = 0.1
exp2_scale = HD ** (-0.5) * math.log2(math.e)


def route(value, target):
    pairs = []
    for source in range(NX * NG * NT):
        ctx, t = divmod(source, NT)
        x, g = divmod(ctx, NG)
        z, y = divmod(g, NY)
        nx, nz, ny, nt = target(x, z, y, t)
        pairs.append((source, (((nx % NX) * NZ + nz % NZ) * NY + ny % NY) * NT + nt % NT))
    return lax.ppermute(value, ("ctx", "tp"), pairs)


def together(*values):
    return lax.optimization_barrier(values)


def pick(value, index, axis=0):
    return lax.dynamic_index_in_dim(value, index, axis, keepdims=False)


def segment_ids(lengths_row, position):
    doc_ends = jnp.cumsum(lengths_row)
    return jnp.sum((position[:, None] >= doc_ends[None, :]).astype(jnp.int32), axis=1)


def group_advantage(rewards, groups):
    flat_reward = rewards.reshape(-1)
    flat_group = groups.reshape(-1)
    same_group = (flat_group[:, None] == flat_group[None, :]).astype(jnp.float32)
    group_mean = jnp.sum(same_group * flat_reward[None, :], axis=1) / jnp.sum(same_group, axis=1)
    return (flat_reward - group_mean).reshape(rewards.shape)


def token_coef(own_advantage, segment, policy_logp, sample_logp, frozen_logp, divisor):
    labels = jnp.arange(own_advantage.shape[0], dtype=jnp.int32)
    picked = jnp.sum(
        jnp.where(segment[:, None] == labels[None, :], own_advantage[None, :], 0.0), axis=1
    )
    return (
        -jnp.exp(policy_logp - sample_logp) * picked
        + kl_weight * (1.0 - jnp.exp(frozen_logp - policy_logp))
    ) / divisor


def in_smem():
    return pl.BlockSpec(memory_space=pltpu.SMEM)


def in_vmem():
    return pl.BlockSpec(memory_space=pltpu.VMEM)


def attention_kernel(where_ref, *refs):
    block_refs, key_refs, refs = refs[:NX], refs[NX : NX + NG], refs[NX + NG :]
    out_ref, keys_ref, query_columns, dout_rows, scores, sums, powers_sum = refs
    g, bound, own = where_ref[0], where_ref[1], where_ref[2]
    for dz in range(NZ):
        for dy in range(NY):
            part = key_refs[dz * NY + dy]
            part_g = lax.rem(g // NY - dz + NZ, NZ) * NY + lax.rem(g - dy + NG, NY)
            for d in range(NX):
                part_x = lax.rem(own - d + NX, NX)
                rows = pl.ds(pl.multiple_of((part_x * NG + part_g) * BLOCK, BLOCK), BLOCK)
                keys_ref[rows, :] = part[d]
    for slot in range(NX):
        for h in range(GROUP):
            rows = pl.ds(h * BLOCK, BLOCK)
            query_columns[slot, :, rows] = block_refs[slot][:, pl.ds(h * HD, HD)].T
            dout_rows[slot, rows, :] = block_refs[slot][:, pl.ds((GROUP + h) * HD, HD)]
    sums[...] = jnp.zeros_like(sums)

    def key_norm(i, longest):
        rows = pl.ds(pl.multiple_of(i * CHUNK, CHUNK), CHUNK)
        block = keys_ref[rows, :].astype(jnp.float32)
        norms = jnp.sum(block * block, axis=1, keepdims=True)
        return jnp.maximum(longest, jnp.max(norms, axis=0, keepdims=True))

    longest_key = lax.fori_loop(0, SLAB // CHUNK, key_norm, jnp.zeros((1, 1), jnp.float32))

    def one_block(slot, _):
        block_start = (lax.rem(own - slot + NX, NX) * NG + g) * BLOCK
        latest_from = jnp.where(block_start + BLOCK - 1 >= bound, bound, 0)
        first = jnp.where(block_start >= bound, bound, 0) // CHUNK
        stop = (block_start + BLOCK - 1) // CHUNK + 1
        block_queries, block_douts = query_columns[slot], dout_rows[slot]

        def scored(rows):
            return jnp.dot(keys_ref[rows, :], block_queries, preferred_element_type=jnp.float32)

        def is_visible(start):
            key_at = start + lax.broadcasted_iota(jnp.int32, (CHUNK, ROWS), 0)
            query_at = block_start + (lax.broadcasted_iota(jnp.int32, (1, ROWS), 1) & (BLOCK - 1))
            from_at = jnp.where(query_at >= bound, bound, 0)
            return (key_at <= query_at) & (key_at >= from_at)

        def by_tile(value):
            return value.reshape(CHUNK // 8, 8, ROWS)

        def add_powers(rows, powers):
            scores[rows, :] = powers
            powers_sum[...] += jnp.sum(by_tile(powers), axis=0)

        as_float = block_queries.astype(jnp.float32)
        norms = jnp.sum(as_float * as_float, axis=0, keepdims=True)
        limit = jnp.sqrt(norms * longest_key) * (1.001 * exp2_scale)
        powers_sum[...] = jnp.zeros_like(powers_sum)

        def from_limit(chunk, _):
            start = pl.multiple_of(chunk * CHUNK, CHUNK)
            rows = pl.ds(start, CHUNK)
            whole = (start + CHUNK - 1 <= block_start) & (start >= latest_from)

            @pl.when(whole)
            def _():
                add_powers(rows, jnp.exp2(scored(rows) * exp2_scale - limit))

            @pl.when(jnp.logical_not(whole))
            def _():
                powers = jnp.exp2(scored(rows) * exp2_scale - limit)
                add_powers(rows, jnp.where(is_visible(start), powers, 0.0))

            return 0

        lax.fori_loop(first, stop, from_limit, 0)

        total = jnp.sum(powers_sum[...], axis=0, keepdims=True)
        kept = jnp.min(jnp.where(total >= 2.0**-60, 1.0, 0.0))

        @pl.when(kept < 0.5)
        def _():
            def masked(chunk, row_max):
                start = pl.multiple_of(chunk * CHUNK, CHUNK)
                rows = pl.ds(start, CHUNK)
                scores[rows, :] = jnp.where(is_visible(start), scored(rows), LOWEST)
                return jnp.maximum(row_max, jnp.max(by_tile(scores[rows, :]), axis=0))

            row_max = lax.fori_loop(first, stop, masked, jnp.full((8, ROWS), LOWEST, jnp.float32))
            row_max = jnp.max(row_max, axis=0, keepdims=True) * exp2_scale
            powers_sum[...] = jnp.zeros_like(powers_sum)

            def from_maximum(chunk, _):
                rows = pl.ds(pl.multiple_of(chunk * CHUNK, CHUNK), CHUNK)
                add_powers(rows, jnp.exp2(scores[rows, :] * exp2_scale - row_max))
                return 0

            lax.fori_loop(first, stop, from_maximum, 0)

        inverse = 1.0 / jnp.sum(powers_sum[...], axis=0, keepdims=True)

        def added(chunk, _):
            rows = pl.ds(pl.multiple_of(chunk * CHUNK, CHUNK), CHUNK)
            sums[rows, :] += jnp.dot(
                (scores[rows, :] * inverse).astype(jnp.bfloat16),
                block_douts,
                preferred_element_type=jnp.float32,
            )
            return 0

        return lax.fori_loop(first, stop, added, 0)

    lax.fori_loop(0, NX, one_block, 0)
    for x in range(NX):
        for y in range(NY):
            for z in range(NZ):
                rows = pl.ds(((x * NZ + z) * NY + y) * BLOCK, BLOCK)
                out_ref[x * NY + y, z] = sums[rows, :].astype(out_ref.dtype)


def attention_terms(where, blocks, keys):
    return pl.pallas_call(
        attention_kernel,
        out_shape=jax.ShapeDtypeStruct((NX * NY, NZ, BLOCK, HD), jnp.bfloat16),
        in_specs=[in_smem()] + [in_vmem()] * (NX + NG),
        out_specs=in_vmem(),
        scratch_shapes=[
            pltpu.VMEM((SLAB, HD), jnp.bfloat16),
            pltpu.VMEM((NX, HD, ROWS), jnp.bfloat16),
            pltpu.VMEM((NX, ROWS, HD), jnp.bfloat16),
            pltpu.VMEM((SLAB, ROWS), jnp.float32),
            pltpu.VMEM((SLAB, HD), jnp.float32),
            pltpu.VMEM((8, ROWS), jnp.float32),
        ],
        compiler_params=pltpu.CompilerParams(vmem_limit_bytes=48 * 1024 * 1024),
        cost_estimate=pl.CostEstimate(
            flops=SLAB, bytes_accessed=SLAB, transcendentals=0
        ),
        name="attention_terms",
    )(where, *blocks, *keys)


def gradient_kernel(where_ref, dvalue_ref, h0_ref, h1_ref, h2_ref, h3_ref, out_ref):
    t = where_ref[3]
    hidden = jnp.concatenate([h0_ref[...], h1_ref[...], h2_ref[...], h3_ref[...]], axis=0)
    matching = jnp.concatenate([dvalue_ref[t ^ d].T for d in range(NX)], axis=1)
    by_column = jnp.dot(matching, hidden, preferred_element_type=jnp.float32)
    out_ref[...] = by_column.T.astype(out_ref.dtype)


def gradient_terms(where, dvalue, hidden_parts):
    width, tile = hidden_parts[0].shape[1], 1280
    columns = pl.BlockSpec((BLOCK, tile), lambda i: (0, i))
    return pl.pallas_call(
        gradient_kernel,
        grid=(width // tile,),
        out_shape=jax.ShapeDtypeStruct((width, HD), jnp.bfloat16),
        in_specs=[
            in_smem(),
            pl.BlockSpec((NX, BLOCK, HD), lambda i: (0, 0, 0)),
        ]
        + [columns] * NX,
        out_specs=pl.BlockSpec((tile, HD), lambda i: (i, 0)),
        cost_estimate=pl.CostEstimate(
            flops=2 * NX * BLOCK * width * HD, bytes_accessed=7 << 20, transcendentals=0
        ),
        name="gradient_terms",
    )(where, dvalue, *hidden_parts)


def copy_kernel(from_ref, to_ref):
    to_ref[...] = from_ref[...]


def copied(value):
    tile = pl.BlockSpec((value.shape[0] // 4, value.shape[1]), lambda i: (i, 0))
    return pl.pallas_call(
        copy_kernel,
        grid=(4,),
        in_specs=[tile],
        out_specs=tile,
        out_shape=jax.ShapeDtypeStruct(value.shape, value.dtype),
        cost_estimate=pl.CostEstimate(
            flops=0, bytes_accessed=4 * value.size, transcendentals=0
        ),
        name="copied",
    )(value)


def decode_weights(dec_query, dec_key, cache_keys, cache_len):
    step_count, row_total = dec_query.shape[:2]
    cache_rows = cache_keys.shape[1]
    score_scale = HD ** (-0.5)
    query_heads = dec_query.reshape(step_count, row_total, GROUP, HD)
    old_scores = (
        jnp.einsum("srgd,rcd->srgc", query_heads, cache_keys, preferred_element_type=jnp.float32)
        * score_scale
    )
    new_scores = (
        jnp.einsum("srgd,jrd->srgj", query_heads, dec_key, preferred_element_type=jnp.float32)
        * score_scale
    )
    old_visible = (jnp.arange(cache_rows, dtype=jnp.int32)[None, :] < cache_len[:, None])[
        None, :, None, :
    ]
    step_ids = jnp.arange(step_count, dtype=jnp.int32)
    new_visible = (step_ids[None, :] <= step_ids[:, None])[:, None, None, :]
    row_max = jnp.maximum(
        jnp.max(jnp.where(old_visible, old_scores, -jnp.inf), axis=3),
        jnp.max(jnp.where(new_visible, new_scores, -jnp.inf), axis=3),
    )[..., None]
    old_exp = jnp.where(old_visible, jnp.exp(old_scores - row_max), 0.0)
    new_exp = jnp.where(new_visible, jnp.exp(new_scores - row_max), 0.0)
    denom = jnp.sum(old_exp, axis=3, keepdims=True) + jnp.sum(new_exp, axis=3, keepdims=True)
    old_weights = (old_exp / denom).astype(jnp.bfloat16)
    new_weights = (new_exp / denom).astype(jnp.bfloat16)
    return old_weights, new_weights


def shards(
    queries,
    attn_keys,
    hidden,
    out_grad,
    logp_new,
    logp_old,
    logp_ref,
    lengths,
    rewards,
    groups,
    master,
    first_moment,
    second_moment,
    dec_hidden,
    dec_query,
    dec_key,
    cache_keys,
    cache_values,
    cache_len,
    out_weight,
):
    bf, f32 = jnp.bfloat16, jnp.float32
    ctx = lax.axis_index("ctx")
    t = lax.axis_index("tp")
    x, g = ctx // NG, ctx % NG
    z, y = g // NY, g % NY

    def exchange(value, groups=None):
        return lax.all_to_all(
            value, "ctx", split_axis=0, concat_axis=0, axis_index_groups=groups, tiled=True
        )

    query_position = ctx * BLOCK + jnp.arange(BLOCK, dtype=jnp.int32)
    query_segment = segment_ids(lengths[0], query_position)
    own_advantage = pick(group_advantage(rewards, groups), t)
    token_weight = token_coef(
        own_advantage, query_segment, logp_new[0], logp_old[0], logp_ref[0], float(rewards.size)
    )
    dout_rows = (token_weight[:, None] * out_grad[0].astype(f32)).astype(bf)

    def along_x(d):
        return lambda x, z, y, t: (x + d, z, y, t)

    def for_head(head):
        width = GROUP * HD
        return jnp.concatenate(
            [
                lax.dynamic_slice_in_dim(queries[0], head * width, width, 1),
                lax.dynamic_slice_in_dim(dout_rows, head * width, width, 1),
            ],
            axis=1,
        )

    sent = [for_head((x + d) % NX) for d in range(NX)]
    def along_z(d):
        return lambda x, z, y, t: (x, z + d, y, t)

    def along_y(x, z, y, t):
        return (x, z, y + 1, t)

    key_heads = attn_keys[0].reshape(BLOCK, KV, HD)
    own_part = jnp.stack(
        [pick(key_heads, x, 1)]
        + [route(pick(key_heads, (x + d) % NX, 1), along_x(d)) for d in range(1, NX)]
    )
    blocks = [sent[0]] + [route(sent[d], along_x(d)) for d in range(1, NX)]
    z_parts = [own_part] + [route(own_part, along_z(d)) for d in range(1, NZ)]
    keys = [part for own in z_parts for part in (own, route(own, along_y))]

    def owner(x, z, y, s, head):
        return (x, s + 2 * (head // 2), y, head)

    def near(x, z, y, t):
        return owner(x, z, y, t, z ^ 1)

    def far(x, z, y, t):
        return owner(x, z, y, t, z ^ 3)

    def swap(x, z, y, t):
        return owner(z, z, y, t, x)

    def flip_core(x, z, y, t):
        return (x, z, y, t ^ 1)

    def flip_chip(x, z, y, t):
        return (x, z, y, t ^ 2)

    own_rows = hidden[0]
    hidden_parts = [None, route(own_rows, near), None, route(own_rows, far)]

    where = jnp.stack([g, lengths[0, 0], x, t]).astype(jnp.int32)
    partial = attention_terms(where, blocks, keys)

    along_zy = [[a * NG + b for b in range(NG)] for a in range(NX)]
    terms = exchange(partial.reshape(NG, NZ * BLOCK, HD), along_zy)
    terms, hidden_parts[1], hidden_parts[3] = together(terms, hidden_parts[1], hidden_parts[3])
    hidden_parts[0] = route(hidden_parts[1], flip_core)
    hidden_parts[2] = route(hidden_parts[3], flip_core)
    dvalue = jnp.sum(terms.astype(f32), axis=0).astype(bf).reshape(NZ, BLOCK, HD)
    dvalue = route(dvalue, swap)
    gradient = gradient_terms(where, dvalue, hidden_parts)
    gradient, dec_query, *state = together(
        gradient, dec_query, master, first_moment, second_moment
    )

    state = jnp.stack(state).reshape(3, 40, KV, HD)

    def over_tp(d):
        return lambda x, z, y, t: (x, z, y, t ^ d)

    moved = [pick(state, t, 2)] + [
        route(pick(state, t ^ d, 2), over_tp(d)) for d in range(1, NT)
    ]
    moved = jnp.stack(moved)
    by_row = jnp.stack([pick(moved, t ^ d) for d in range(NT)], axis=1)
    old_master, old_first, old_second = by_row.reshape(3, NT * 40, HD)

    old_weights, new_weights = decode_weights(dec_query, dec_key, cache_keys, cache_len)
    terms = exchange(gradient.reshape(NX * NG, NT * 40, HD))
    gradient = jnp.sum(terms.astype(f32), axis=0)

    new_first = first_decay * old_first + (1.0 - first_decay) * gradient
    new_second = second_decay * old_second + (1.0 - second_decay) * gradient * gradient
    new_master = old_master - learn_rate * (
        new_first / (jnp.sqrt(new_second) + adam_eps) + decay_weight * old_master
    )
    cached = jnp.einsum(
        "srgc,rcd->srgd", old_weights, cache_values, preferred_element_type=f32
    )
    rounded, cached, new_weights, out_weight = together(
        new_master.astype(bf), cached, new_weights, out_weight
    )
    core, half = t % 2, out_weight.shape[1] // 2
    own_weight = lax.dynamic_slice_in_dim(out_weight, core * half, half, 1)
    other_weight = lax.dynamic_slice_in_dim(out_weight, (1 - core) * half, half, 1)
    rollout = exchange(jnp.broadcast_to(rounded[None], (NX * NG, NT * 40, HD))).reshape(5120, HD)

    news = jnp.stack([new_master, new_first, new_second]).reshape(3, NT, 40, HD)
    back = [pick(news, t, 1)] + [
        route(pick(news, t ^ d, 1), over_tp(d)) for d in range(1, NT)
    ]
    back = jnp.stack(back)
    back = jnp.stack([pick(back, t ^ d) for d in range(NT)], axis=2)
    rollout, back, own_weight, other_weight = together(rollout, back, own_weight, other_weight)
    new_master, new_first, new_second = back.reshape(3, 40, KV * HD)

    step_count, dec_rows = dec_hidden.shape[:2]
    rows = step_count * dec_rows
    fresh = jnp.dot(
        dec_hidden.reshape(rows, dec_hidden.shape[2]), rollout, preferred_element_type=f32
    )
    fresh = fresh.reshape(step_count, dec_rows, HD).astype(bf).astype(f32)
    attended = cached
    for j in range(step_count):
        attended = attended + new_weights[..., j : j + 1].astype(f32) * fresh[j][None, :, None, :]
    attended = attended.astype(bf).reshape(rows, GROUP * HD)

    received = route(jnp.dot(attended, other_weight, preferred_element_type=f32), flip_core)
    (own_out,) = together(jnp.dot(attended, own_weight, preferred_element_type=f32))
    on_chip = own_out + received
    from_chip, rollout = together(route(on_chip.astype(bf), flip_chip), copied(rollout))
    both = (on_chip + from_chip.astype(f32)).astype(bf)
    rest = route(both, flip_core)
    dec_out = jnp.zeros((rows, 2 * half), bf)
    dec_out = lax.dynamic_update_slice_in_dim(dec_out, both, core * half, 1)
    dec_out = lax.dynamic_update_slice_in_dim(dec_out, rest, (1 - core) * half, 1)
    dec_out = dec_out.reshape(step_count, dec_rows, 2 * half)
    return (new_master, new_first, new_second, rollout, dec_out)


def solution(mesh):
    return jax.shard_map(
        shards,
        mesh=mesh,
        in_specs=(
            P("tp", "ctx", None),
            P("tp", "ctx", None),
            P("tp", "ctx", None),
            P("tp", "ctx", None),
            P("tp", "ctx"),
            P("tp", "ctx"),
            P("tp", "ctx"),
            P("tp", None),
            P(),
            P(),
            P(("ctx", "tp"), None),
            P(("ctx", "tp"), None),
            P(("ctx", "tp"), None),
            P(None, "ctx", None),
            P(None, "ctx", "tp"),
            P(None, "ctx", "tp"),
            P("ctx", None, "tp"),
            P("ctx", None, "tp"),
            P("ctx"),
            P("tp", None),
        ),
        out_specs=(
            P(("ctx", "tp"), None),
            P(("ctx", "tp"), None),
            P(("ctx", "tp"), None),
            P(None, "tp"),
            P(None, "ctx", None),
        ),
        check_vma=False,
    )
```
